32 devices in a mesh: groups: 2 (over y), ctx: 4 (over x, core), head: 4 (over z).
Axes of the slice: x: 2, y: 2, z: 4, core: 2. Of those that a mesh axis runs over, the one named last changes fastest.
Arguments:
- queries: bfloat16 [384, 64, 128], P(('groups', 'ctx'), 'head'), parts along dimension 0, may hold values from -16 to 16
- prefix_keys: bfloat16 [16384, 8, 128], P(('groups', 'ctx'), 'head'), parts along dimension 0, may hold values from -16 to 16
- prefix_values: bfloat16 [16384, 8, 128], P(('groups', 'ctx'), 'head'), parts along dimension 0, may hold values from -12 to 12
- suffix_keys: bfloat16 [384, 512, 8, 128], P(('groups', 'ctx'), None, 'head'), parts along dimension 0, may hold values from -16 to 16
- suffix_values: bfloat16 [384, 512, 8, 128], P(('groups', 'ctx'), None, 'head'), parts along dimension 0, may hold values from -12 to 12
- lengths: int32 [384], P(('groups', 'ctx')), parts along dimension 0, may hold values from 1 to 512, as said below
Outputs:
- attended: bfloat16 [384, 64, 128], P(('groups', 'ctx'), 'head'), parts along dimension 0
The draws below stay inside these ranges and needn't reach their ends.
There are 2 independent parts, one for each index of `groups`. The reference program is written for one: setup_inputs(seed, part) draws one part's arguments, and reference() takes and returns one part's arrays. A program takes and returns all parts, laid end to end along the dimension named above; each array names one. Nothing has to cross between parts.
Inputs may be any that keep to these rules, and one draw needn't show every extreme that they name: The live slots of a row are its first lengths[r] slots; some row of each part has exactly 512.
All inputs are finite; a program needn't handle non-finite values.
Results may differ from the reference program's by a relative error of at most 0.0025.
Values may be sent and summed in bfloat16 or wider, within the bound.
No kernel may reach another device: no remote copies, remote signals or barrier semaphores. Data moves between devices by JAX's collectives and lax.ppermute only.
A program may use at most 128 MiB of HBM per device.

```python
import math
import jax
import jax.numpy as jnp
from jax import lax

Q_HEADS = 64
KV_HEADS = 8
HEAD_DIM = 128
ROWS_DEV = 48
PREFIX_DEV = 2048
SUFFIX = 512
ROWS = 192
PREFIX = 8192
N_CTX = 4


def draw_queries(key, part):
    key_base = jax.random.fold_in(key, 1)
    base_draw = jnp.clip(jax.random.normal(key_base, (ROWS, Q_HEADS, HEAD_DIM), jnp.float32), -5.0, 5.0)
    return base_draw.astype(jnp.bfloat16)


def draw_prefix_keys(key, part):
    key_base = jax.random.fold_in(key, 2)
    base_draw = jnp.clip(2.5 * jax.random.normal(key_base, (PREFIX, KV_HEADS, HEAD_DIM), jnp.float32), -15.0, 15.0)
    return base_draw.astype(jnp.bfloat16)


def draw_lengths(key, part):
    key_level, key_raw, key_long = jax.random.split(jax.random.fold_in(key, 5), 3)
    block_count = ROWS // ROWS_DEV
    levels = jax.random.randint(key_level, (block_count,), 1, 9)
    ceiling = jnp.repeat(SUFFIX * levels // 8, ROWS_DEV, total_repeat_length=ROWS)
    raw_draw = jax.random.randint(key_raw, (ROWS,), 0, SUFFIX)
    result = 1 + raw_draw % ceiling
    longest = jax.random.randint(key_long, (), 0, ROWS)
    result = result.at[longest].set(SUFFIX)
    return result.astype(jnp.int32)


def block_levels(rng, shape, cuts, low, high):
    loudness = 1.0
    for position, shards_of in cuts:
        draws = jax.random.uniform(jax.random.fold_in(jax.random.fold_in(rng, 6), position), (shards_of,), jnp.float32, low / len(cuts), high / len(cuts))
        loudness = loudness * jnp.repeat(jnp.exp(draws), shape[position] // shards_of).reshape((-1,) + (1,) * (len(shape) - 1 - position))
    return loudness


def normal_values(stream_key, dims, deviation, limit, cuts=(), kind=jnp.bfloat16):
    array = jax.random.normal(stream_key, dims, jnp.float32) * deviation
    if len(cuts) > 0:
        array = block_levels(stream_key, dims, cuts, -0.22, 0.18) * array
    return jnp.clip(array, min=-limit, max=limit).astype(kind)


def setup_inputs(seed: int = 0, part: int = 0) -> dict:
    streams_of = jax.random.split(jax.random.key(seed), 7)
    part_splits = jax.random.split(jax.random.fold_in(streams_of[6], part), 7)
    queries = draw_queries(jax.random.fold_in(jax.random.fold_in(streams_of[6], part), 71), part)
    prefix_keys = draw_prefix_keys(jax.random.fold_in(jax.random.fold_in(streams_of[6], part), 71), part)
    prefix_values = normal_values(part_splits[2], (PREFIX, KV_HEADS, HEAD_DIM), 2.0, 12.0, ((0, 4), (1, 4)))
    suffix_keys = normal_values(part_splits[3], (ROWS, SUFFIX, KV_HEADS, HEAD_DIM), 4.0, 16.0, ((0, 4), (2, 4)))
    suffix_values = normal_values(part_splits[4], (ROWS, SUFFIX, KV_HEADS, HEAD_DIM), 2.0, 12.0, ((0, 4), (2, 4)))
    lengths = draw_lengths(jax.random.fold_in(jax.random.fold_in(streams_of[6], part), 71), part)
    return {"queries": queries, "prefix_keys": prefix_keys, "prefix_values": prefix_values, "suffix_keys": suffix_keys, "suffix_values": suffix_values, "lengths": lengths}


def reference(queries, prefix_keys, prefix_values, suffix_keys, suffix_values, lengths):
    rows, heads, head_width = queries.shape
    kv_count = prefix_keys.shape[1]
    group_size = heads // kv_count
    span = suffix_keys.shape[1]
    scaling = head_width ** -0.5
    keys_wide = prefix_keys.astype(jnp.float32)
    values_wide = prefix_values.astype(jnp.float32).reshape(N_CTX, PREFIX_DEV, kv_count, head_width)
    positions = jnp.arange(span, dtype=jnp.int32)
    block_rows = math.gcd(rows, 8)
    count_blocks = rows // block_rows

    def one_block(pieces):
        query_block, keys_block, values_block, length_block = pieces
        grouped = query_block.astype(jnp.float32).reshape(block_rows, kv_count, group_size, head_width)
        prefix_part = jnp.einsum("rkgd,pkd->rkgp", grouped, keys_wide, precision=lax.Precision.HIGHEST) * scaling
        prefix_part = prefix_part.reshape(block_rows, kv_count, group_size, N_CTX, PREFIX_DEV)
        suffix_part = jnp.einsum("rkgd,rskd->rkgs", grouped, keys_block.astype(jnp.float32), precision=lax.Precision.HIGHEST) * scaling
        live_mask = (positions[None, :] < length_block[:, None])[:, None, None, :]
        block_top = jnp.max(prefix_part, axis=-1)
        row_top = jnp.maximum(jnp.max(block_top, axis=-1), jnp.max(jnp.where(live_mask, suffix_part, -jnp.inf), axis=-1))
        prefix_weights = jnp.exp(prefix_part - block_top[..., None]).astype(jnp.bfloat16)
        block_scale = jnp.exp(block_top - row_top[..., None])
        suffix_weights = jnp.where(live_mask, jnp.exp(suffix_part - row_top[..., None]), 0.0).astype(jnp.bfloat16)
        prefix_float = prefix_weights.astype(jnp.float32)
        suffix_float = suffix_weights.astype(jnp.float32)
        weight_sum = jnp.sum(jnp.sum(prefix_float, axis=-1) * block_scale, axis=-1) + jnp.sum(suffix_float, axis=-1)
        partial_accum = jnp.einsum("rkgcp,cpkd->rkgcd", prefix_float, values_wide, precision=lax.Precision.HIGHEST)
        accumulated = jnp.sum(partial_accum * block_scale[..., None], axis=-2)
        accumulated = accumulated + jnp.einsum("rkgs,rskd->rkgd", suffix_float, values_block.astype(jnp.float32), precision=lax.Precision.HIGHEST)
        result = (accumulated / weight_sum[..., None]).astype(jnp.bfloat16)
        return result.reshape(block_rows, heads, head_width)

    stacked = lax.map(one_block, (
        queries.reshape(count_blocks, block_rows, heads, head_width),
        suffix_keys.reshape(count_blocks, block_rows, span, kv_count, head_width),
        suffix_values.reshape(count_blocks, block_rows, span, kv_count, head_width),
        lengths.reshape(count_blocks, block_rows)))
    return stacked.reshape(rows, heads, head_width)
```

```python
from functools import partial

import jax
import jax.numpy as jnp
from jax import lax
from jax.experimental import pallas as pl
from jax.experimental.pallas import tpu as pltpu
from jax.sharding import PartitionSpec as P

LOG2E = 1.4426950408889634
F32 = jnp.float32
BF16 = jnp.bfloat16
VMEM = pl.BlockSpec(memory_space=pltpu.VMEM)


def split_heads(q_ref, kv_heads):
    rows, heads, d = q_ref.shape
    group = heads // kv_heads
    wide = q_ref[...].astype(F32)
    return [
        wide[:, h * group : (h + 1) * group, :].reshape(rows * group, d).astype(BF16)
        for h in range(kv_heads)
    ]


def block_attend(q, k, v, c):
    s = lax.dot_general(q, k, (((1,), (1,)), ((), ())), preferred_element_type=F32)
    top = jnp.max(s, axis=1, keepdims=True)
    w = jnp.exp2(s * c - top * c).astype(BF16)
    va = jnp.concatenate([v, jnp.ones_like(v)], axis=1)
    oa = jnp.dot(w, va, preferred_element_type=F32)
    d = v.shape[1]
    return oa[:, :d], oa[:, d:], top * c


def attend_blocks(q, blocks, c):
    parts = [block_attend(q, k, v, c) for k, v in blocks]
    top = parts[0][2]
    for part in parts[1:]:
        top = jnp.maximum(top, part[2])
    acc = 0.0
    total = 0.0
    for o, l, t in parts:
        scale = jnp.exp2(t - top)
        acc = acc + o * scale
        total = total + l * scale
    return acc / total, top + jnp.log2(total)


def lane_eye(n):
    return lax.broadcasted_iota(jnp.int32, (n, n), 0) == lax.broadcasted_iota(jnp.int32, (n, n), 1)


def other_kernel(q_ref, *refs, c, kv_heads, pieces):
    kv_refs, msg_ref = refs[:-1], refs[-1]
    heads_q = split_heads(q_ref, kv_heads)
    m, d = heads_q[0].shape
    eye = lane_eye(d)
    packed = []
    for h in range(kv_heads):
        blocks = [(kv_refs[2 * b][h], kv_refs[2 * b + 1][h]) for b in range(len(kv_refs) // 2)]
        o, lse = attend_blocks(heads_q[h], blocks, c)
        msg_ref[h * m : (h + 1) * m, :] = o.astype(BF16)
        packed.append(jnp.sum(jnp.where(eye, lse.reshape(m // d, d, d), 0.0), axis=1))
    rest = jnp.concatenate(packed, axis=0)
    out = []
    for _ in range(3):
        piece = rest.astype(BF16).astype(F32)
        out.append(piece)
        rest = rest - piece
    used = 3 * out[0].shape[0]
    if pieces > used:
        out.append(jnp.zeros((pieces - used, d), F32))
    msg_ref[kv_heads * m :, :] = jnp.concatenate(out, axis=0).astype(BF16)


def own_kernel(q_ref, *refs, c, kv_heads):
    kv_refs, o_ref, lse_ref = refs[:-2], refs[-2], refs[-1]
    heads_q = split_heads(q_ref, kv_heads)
    for h in range(kv_heads):
        blocks = [(kv_refs[2 * b][h], kv_refs[2 * b + 1][h]) for b in range(len(kv_refs) // 2)]
        o, lse = attend_blocks(heads_q[h], blocks, c)
        o_ref[h] = o
        lse_ref[h] = lse


def suffix_kernel(len_ref, q_ref, k_hbm, v_hbm, o_ref, lse_ref, kb, vb, ksem, vsem, *, c, kv_heads, batch):
    rows, heads, d = q_ref.shape
    group = heads // kv_heads
    slots = kb.shape[1]
    lane = lax.broadcasted_iota(jnp.int32, (heads, slots), 1)
    head = lax.broadcasted_iota(jnp.int32, (heads, slots), 0) // group
    place = jnp.where(lane % kv_heads == head, lane // kv_heads, slots)

    def keys(r):
        return pltpu.make_async_copy(k_hbm.at[r], kb.at[r], ksem.at[r])

    def values(r):
        return pltpu.make_async_copy(v_hbm.at[r], vb.at[r], vsem.at[r])

    def issue(r, _):
        keys(r).start()
        values(r).start()
        return 0

    lax.fori_loop(0, rows, issue, 0)

    def body(i, _):
        base = i * batch
        scores = []
        for j in range(batch):
            keys(base + j).wait()
        for j in range(batch):
            r = base + j
            s = lax.dot_general(q_ref[r], kb[r], (((1,), (1,)), ((), ())), preferred_element_type=F32)
            scores.append(jnp.where(place < len_ref[r], s, -jnp.inf))
        weights = []
        for j in range(batch):
            top = jnp.max(scores[j], axis=1, keepdims=True)
            w = jnp.exp2(scores[j] * c - top * c).astype(BF16)
            total = jnp.sum(w.astype(F32), axis=1, keepdims=True)
            weights.append((w, top * c, total))
        for j in range(batch):
            values(base + j).wait()
        for j in range(batch):
            r = base + j
            w, top, total = weights[j]
            o = jnp.dot(w, vb[r], preferred_element_type=F32)
            o_ref[r] = o / total
            lse_ref[r] = jnp.broadcast_to(top + jnp.log2(total), (heads, d))
        return 0

    lax.fori_loop(0, rows // batch, body, 0)


def merge_kernel(os_ref, ls_ref, op_ref, lp_ref, *refs, kv_heads, group):
    msg_refs, out_ref = refs[:-1], refs[-1]
    rows, heads, d = os_ref.shape
    m = rows * group
    n = m // d
    eye = lane_eye(d)
    results = []
    for h in range(kv_heads):
        cols = slice(h * group, (h + 1) * group)
        parts = [
            (os_ref[:, cols, :].reshape(m, d), ls_ref[:, cols, :].reshape(m, d)),
            (op_ref[h], lp_ref[h]),
        ]
        for msg in msg_refs:
            o = msg[h * m : (h + 1) * m, :].astype(F32)
            tail = msg[kv_heads * m :, :].astype(F32)
            lse = sum(tail[(p * kv_heads + h) * n : (p * kv_heads + h + 1) * n] for p in range(3))
            lse = jnp.where(eye, jnp.broadcast_to(lse[:, None, :], (n, d, d)), 0.0)
            lse = jnp.sum(lse, axis=2, keepdims=True).reshape(m, 1)
            parts.append((o, jnp.broadcast_to(lse, (m, d))))
        top = parts[0][1]
        for part in parts[1:]:
            top = jnp.maximum(top, part[1])
        acc = 0.0
        total = 0.0
        for o, l in parts:
            w = jnp.exp2(l - top)
            acc = acc + o * w
            total = total + w
        results.append((acc / total).reshape(rows, group, d))
    out_ref[...] = jnp.concatenate(results, axis=1).astype(BF16)


def shards(queries, prefix_keys, prefix_values, suffix_keys, suffix_values, lengths):
    rows, heads, d = queries.shape
    kv_heads = prefix_keys.shape[1]
    group = heads // kv_heads
    span = suffix_keys.shape[1]
    c = d ** (-0.5) * LOG2E
    n = lax.axis_size("ctx")
    cores = 2 if n % 2 == 0 else 1
    chips = n // cores
    m = rows * group
    pieces = -(-3 * kv_heads * (m // d) // 16) * 16

    def shift(x, by):
        return lax.ppermute(x, "ctx", [(i, (i + by) % n) for i in range(n)])

    def call(kernel, out_shape, operands, specs, scratch=(), mib=40, name=None, flops=0, moved=0):
        single = not isinstance(out_shape, tuple)
        return pl.pallas_call(
            kernel,
            out_shape=out_shape,
            in_specs=specs,
            out_specs=VMEM if single else (VMEM,) * len(out_shape),
            scratch_shapes=scratch,
            compiler_params=pltpu.CompilerParams(vmem_limit_bytes=mib << 20),
            cost_estimate=pl.CostEstimate(flops=flops, bytes_accessed=moved, transcendentals=0),
            name=name,
        )(*operands)

    kv = [(prefix_keys, prefix_values)]
    if cores == 2:
        swap = [(i, i ^ 1) for i in range(n)]
        kv.append((lax.ppermute(prefix_keys, "ctx", swap), lax.ppermute(prefix_values, "ctx", swap)))
    visiting = [shift(queries, j * cores) for j in range(1, chips)]

    slots = span * kv_heads
    suffix_o, suffix_l = call(
        partial(suffix_kernel, c=c, kv_heads=kv_heads, batch=8 if rows % 8 == 0 else 1),
        (jax.ShapeDtypeStruct((rows, heads, d), F32),) * 2,
        (lengths, queries, suffix_keys.reshape(rows, slots, d), suffix_values.reshape(rows, slots, d)),
        [pl.BlockSpec(memory_space=pltpu.SMEM), VMEM, pl.BlockSpec(memory_space=pl.ANY), pl.BlockSpec(memory_space=pl.ANY)],
        scratch=[
            pltpu.VMEM((rows, slots, d), BF16),
            pltpu.VMEM((rows, slots, d), BF16),
            pltpu.SemaphoreType.DMA((rows,)),
            pltpu.SemaphoreType.DMA((rows,)),
        ],
        mib=40,
        name="suffix",
        flops=4 * rows * heads * slots * d,
        moved=4 * rows * slots * d,
    )

    flat = [x.transpose(1, 0, 2) for pair in kv for x in pair]
    positions = cores * prefix_keys.shape[0]
    flops = 4 * m * kv_heads * positions * d
    message = jax.ShapeDtypeStruct((kv_heads * m + pieces, d), BF16)
    returned = []
    for j, q in enumerate(visiting):
        msg = call(
            partial(other_kernel, c=c, kv_heads=kv_heads, pieces=pieces),
            message,
            (q, *flat),
            [VMEM] * (1 + len(flat)),
            name="visiting",
            flops=flops,
            moved=4 * kv_heads * positions * d,
        )
        returned.append(shift(msg, -(j + 1) * cores))
    own_o, own_l = call(
        partial(own_kernel, c=c, kv_heads=kv_heads),
        (jax.ShapeDtypeStruct((kv_heads, m, d), F32),) * 2,
        (queries, *flat),
        [VMEM] * (1 + len(flat)),
        name="own",
        flops=flops,
        moved=4 * kv_heads * positions * d,
    )
    operands = (suffix_o, suffix_l, own_o, own_l, *returned)
    return call(
        partial(merge_kernel, kv_heads=kv_heads, group=group),
        jax.ShapeDtypeStruct((rows, heads, d), BF16),
        operands,
        [VMEM] * len(operands),
        name="merge",
    )


def solution(mesh):
    placed = (
        P(("groups", "ctx"), "head", None),
        P(("groups", "ctx"), "head", None),
        P(("groups", "ctx"), "head", None),
        P(("groups", "ctx"), None, "head", None),
        P(("groups", "ctx"), None, "head", None),
        P(("groups", "ctx")),
    )
    return jax.shard_map(
        shards,
        mesh=mesh,
        in_specs=placed,
        out_specs=P(("groups", "ctx"), "head", None),
        check_vma=False,
    )
```

```python
from functools import partial

import jax
import jax.numpy as jnp
from jax import lax
from jax.experimental import pallas as pl
from jax.experimental.pallas import tpu as pltpu
from jax.sharding import PartitionSpec as P

LOG2E = 1.4426950408889634
F32 = jnp.float32
BF16 = jnp.bfloat16
VMEM = pl.BlockSpec(memory_space=pltpu.VMEM)


def split_heads(q_ref, kv_heads):
    rows, heads, d = q_ref.shape
    group = heads // kv_heads
    wide = q_ref[...].astype(F32)
    return [
        wide[:, h * group : (h + 1) * group, :].reshape(rows * group, d).astype(BF16)
        for h in range(kv_heads)
    ]


def block_attend(q, k, v, c):
    s = lax.dot_general(q, k, (((1,), (1,)), ((), ())), preferred_element_type=F32)
    top = jnp.max(s, axis=1, keepdims=True)
    w = jnp.exp2(s * c - top * c).astype(BF16)
    va = jnp.concatenate([v, jnp.ones_like(v)], axis=1)
    oa = jnp.dot(w, va, preferred_element_type=F32)
    d = v.shape[1]
    return oa[:, :d], oa[:, d:], top * c


def attend_blocks(q, blocks, c):
    parts = [block_attend(q, k, v, c) for k, v in blocks]
    top = parts[0][2]
    for part in parts[1:]:
        top = jnp.maximum(top, part[2])
    acc = 0.0
    total = 0.0
    for o, l, t in parts:
        scale = jnp.exp2(t - top)
        acc = acc + o * scale
        total = total + l * scale
    return acc / total, top + jnp.log2(total)


def lane_eye(n):
    return lax.broadcasted_iota(jnp.int32, (n, n), 0) == lax.broadcasted_iota(jnp.int32, (n, n), 1)


def other_kernel(q_ref, *refs, c, kv_heads, pieces):
    kv_refs, msg_ref = refs[:-1], refs[-1]
    heads_q = split_heads(q_ref, kv_heads)
    m, d = heads_q[0].shape
    eye = lane_eye(d)
    packed = []
    for h in range(kv_heads):
        blocks = [(kv_refs[2 * b][h], kv_refs[2 * b + 1][h]) for b in range(len(kv_refs) // 2)]
        o, lse = attend_blocks(heads_q[h], blocks, c)
        msg_ref[h * m : (h + 1) * m, :] = o.astype(BF16)
        packed.append(jnp.sum(jnp.where(eye, lse.reshape(m // d, d, d), 0.0), axis=1))
    rest = jnp.concatenate(packed, axis=0)
    out = []
    for _ in range(3):
        piece = rest.astype(BF16).astype(F32)
        out.append(piece)
        rest = rest - piece
    used = 3 * out[0].shape[0]
    if pieces > used:
        out.append(jnp.zeros((pieces - used, d), F32))
    msg_ref[kv_heads * m :, :] = jnp.concatenate(out, axis=0).astype(BF16)


def own_kernel(q_ref, *refs, c, kv_heads):
    kv_refs, o_ref, lse_ref = refs[:-2], refs[-2], refs[-1]
    heads_q = split_heads(q_ref, kv_heads)
    for h in range(kv_heads):
        blocks = [(kv_refs[2 * b][h], kv_refs[2 * b + 1][h]) for b in range(len(kv_refs) // 2)]
        o, lse = attend_blocks(heads_q[h], blocks, c)
        o_ref[h] = o
        lse_ref[h] = lse


def suffix_kernel(len_ref, q_ref, k_hbm, v_hbm, o_ref, lse_ref, kb, vb, ksem, vsem, *, c, kv_heads, batch):
    rows, heads, d = q_ref.shape
    group = heads // kv_heads
    slots = kb.shape[1]
    lane = lax.broadcasted_iota(jnp.int32, (heads, slots), 1)
    head = lax.broadcasted_iota(jnp.int32, (heads, slots), 0) // group
    place = jnp.where(lane % kv_heads == head, lane // kv_heads, slots)

    def keys(r):
        return pltpu.make_async_copy(k_hbm.at[r], kb.at[r], ksem.at[r])

    def values(r):
        return pltpu.make_async_copy(v_hbm.at[r], vb.at[r], vsem.at[r])

    def issue(r, _):
        keys(r).start()
        values(r).start()
        return 0

    lax.fori_loop(0, rows, issue, 0)

    def body(i, _):
        base = i * batch
        scores = []
        for j in range(batch):
            keys(base + j).wait()
        for j in range(batch):
            r = base + j
            s = lax.dot_general(q_ref[r], kb[r], (((1,), (1,)), ((), ())), preferred_element_type=F32)
            scores.append(jnp.where(place < len_ref[r], s, -jnp.inf))
        weights = []
        for j in range(batch):
            top = jnp.max(scores[j], axis=1, keepdims=True)
            w = jnp.exp2(scores[j] * c - top * c).astype(BF16)
            total = jnp.sum(w.astype(F32), axis=1, keepdims=True)
            weights.append((w, top * c, total))
        for j in range(batch):
            values(base + j).wait()
        for j in range(batch):
            r = base + j
            w, top, total = weights[j]
            o = jnp.dot(w, vb[r], preferred_element_type=F32)
            o_ref[r] = o / total
            lse_ref[r] = jnp.broadcast_to(top + jnp.log2(total), (heads, d))
        return 0

    lax.fori_loop(0, rows // batch, body, 0)


def merge_kernel(os_ref, ls_ref, op_ref, lp_ref, *refs, kv_heads, group):
    msg_refs, out_ref = refs[:-1], refs[-1]
    rows, heads, d = os_ref.shape
    m = rows * group
    n = m // d
    eye = lane_eye(d)
    results = []
    for h in range(kv_heads):
        cols = slice(h * group, (h + 1) * group)
        parts = [
            (os_ref[:, cols, :].reshape(m, d), ls_ref[:, cols, :].reshape(m, d)),
            (op_ref[h], lp_ref[h]),
        ]
        for msg in msg_refs:
            o = msg[h * m : (h + 1) * m, :].astype(F32)
            tail = msg[kv_heads * m :, :].astype(F32)
            lse = sum(tail[(p * kv_heads + h) * n : (p * kv_heads + h + 1) * n] for p in range(3))
            lse = jnp.where(eye, jnp.broadcast_to(lse[:, None, :], (n, d, d)), 0.0)
            lse = jnp.sum(lse, axis=2, keepdims=True).reshape(m, 1)
            parts.append((o, jnp.broadcast_to(lse, (m, d))))
        top = parts[0][1]
        for part in parts[1:]:
            top = jnp.maximum(top, part[1])
        acc = 0.0
        total = 0.0
        for o, l in parts:
            w = jnp.exp2(l - top)
            acc = acc + o * w
            total = total + w
        results.append((acc / total).reshape(rows, group, d))
    out_ref[...] = jnp.concatenate(results, axis=1).astype(BF16)


def shards(queries, prefix_keys, prefix_values, suffix_keys, suffix_values, lengths):
    rows, heads, d = queries.shape
    kv_heads = prefix_keys.shape[1]
    group = heads // kv_heads
    span = suffix_keys.shape[1]
    c = d ** (-0.5) * LOG2E
    n = lax.axis_size("ctx")
    cores = 2 if n % 2 == 0 else 1
    chips = n // cores
    m = rows * group
    pieces = -(-3 * kv_heads * (m // d) // 16) * 16

    def shift(x, by):
        return lax.ppermute(x, "ctx", [(i, (i + by) % n) for i in range(n)])

    def call(kernel, out_shape, operands, specs, scratch=(), mib=40, name=None, flops=0, moved=0):
        single = not isinstance(out_shape, tuple)
        return pl.pallas_call(
            kernel,
            out_shape=out_shape,
            in_specs=specs,
            out_specs=VMEM if single else (VMEM,) * len(out_shape),
            scratch_shapes=scratch,
            compiler_params=pltpu.CompilerParams(vmem_limit_bytes=mib << 20),
            cost_estimate=pl.CostEstimate(flops=flops, bytes_accessed=moved, transcendentals=0),
            name=name,
        )(*operands)

    flat = [prefix_keys.reshape(-1, d), prefix_values.reshape(-1, d)]
    if cores == 2:
        swap = [(i, i ^ 1) for i in range(n)]
        flat += [lax.ppermute(x, "ctx", swap) for x in flat]
    visiting = [shift(queries, j * cores) for j in range(1, chips)]

    slots = span * kv_heads
    suffix_o, suffix_l = call(
        partial(suffix_kernel, c=c, kv_heads=kv_heads, batch=8 if rows % 8 == 0 else 1),
        (jax.ShapeDtypeStruct((rows, heads, d), F32),) * 2,
        (lengths, queries, suffix_keys.reshape(rows, slots, d), suffix_values.reshape(rows, slots, d)),
        [pl.BlockSpec(memory_space=pltpu.SMEM), VMEM, pl.BlockSpec(memory_space=pl.ANY), pl.BlockSpec(memory_space=pl.ANY)],
        scratch=[
            pltpu.VMEM((rows, slots, d), BF16),
            pltpu.VMEM((rows, slots, d), BF16),
            pltpu.SemaphoreType.DMA((rows,)),
            pltpu.SemaphoreType.DMA((rows,)),
        ],
        mib=50,
        name="suffix",
        flops=4 * rows * heads * slots * d,
        moved=4 * rows * slots * d,
    )

    visiting, flat, suffix_o, suffix_l = lax.optimization_barrier((visiting, flat, suffix_o, suffix_l))
    flat = [x.reshape(-1, kv_heads, d).transpose(1, 0, 2) for x in flat]
    positions = cores * prefix_keys.shape[0]
    flops = 4 * m * kv_heads * positions * d
    message = jax.ShapeDtypeStruct((kv_heads * m + pieces, d), BF16)
    returned = []
    for j, q in enumerate(visiting):
        msg = call(
            partial(other_kernel, c=c, kv_heads=kv_heads, pieces=pieces),
            message,
            (q, *flat),
            [VMEM] * (1 + len(flat)),
            name="visiting",
            flops=flops,
            moved=4 * kv_heads * positions * d,
        )
        returned.append(shift(msg, -(j + 1) * cores))
    own_o, own_l = call(
        partial(own_kernel, c=c, kv_heads=kv_heads),
        (jax.ShapeDtypeStruct((kv_heads, m, d), F32),) * 2,
        (queries, *flat),
        [VMEM] * (1 + len(flat)),
        name="own",
        flops=flops,
        moved=4 * kv_heads * positions * d,
    )
    operands = (suffix_o, suffix_l, own_o, own_l, *returned)
    return call(
        partial(merge_kernel, kv_heads=kv_heads, group=group),
        jax.ShapeDtypeStruct((rows, heads, d), BF16),
        operands,
        [VMEM] * len(operands),
        name="merge",
    )


def solution(mesh):
    placed = (
        P(("groups", "ctx"), "head", None),
        P(("groups", "ctx"), "head", None),
        P(("groups", "ctx"), "head", None),
        P(("groups", "ctx"), None, "head", None),
        P(("groups", "ctx"), None, "head", None),
        P(("groups", "ctx")),
    )
    return jax.shard_map(
        shards,
        mesh=mesh,
        in_specs=placed,
        out_specs=P(("groups", "ctx"), "head", None),
        check_vma=False,
    )
```

```python
from functools import partial

import jax
import jax.numpy as jnp
from jax import lax
from jax.experimental import pallas as pl
from jax.experimental.pallas import tpu as pltpu
from jax.sharding import PartitionSpec as P

LOG2E = 1.4426950408889634
F32 = jnp.float32
BF16 = jnp.bfloat16
VMEM = pl.BlockSpec(memory_space=pltpu.VMEM)


def split_heads(q_ref, kv_heads):
    rows, heads, d = q_ref.shape
    group = heads // kv_heads
    wide = q_ref[...].astype(F32)
    return [
        wide[:, h * group : (h + 1) * group, :].reshape(rows * group, d).astype(BF16)
        for h in range(kv_heads)
    ]


def scores_of(q, k):
    return lax.dot_general(q, k, (((1,), (1,)), ((), ())), preferred_element_type=F32)


def attend_blocks(heads_q, kv_refs, c):
    d = heads_q[0].shape[1]
    blocks = len(kv_refs) // 2
    items = [(h, b) for h in range(len(heads_q)) for b in range(blocks)]
    parts = {}
    s = w = None
    for step in range(len(items) + 2):
        s_next = w_next = None
        if step < len(items):
            h, b = items[step]
            s_next = scores_of(heads_q[h], kv_refs[2 * b][h])
        if w is not None:
            h, b = items[step - 2]
            v = kv_refs[2 * b + 1][h]
            oa = jnp.dot(w[0], jnp.concatenate([v, jnp.ones_like(v)], axis=1), preferred_element_type=F32)
            parts[h, b] = (oa[:, :d], oa[:, d:], w[1])
        if s is not None:
            top = jnp.max(s, axis=1, keepdims=True)
            w_next = (jnp.exp2(s * c - top * c).astype(BF16), top * c)
        s, w = s_next, w_next
    results = []
    for h in range(len(heads_q)):
        top = parts[h, 0][2]
        for b in range(1, blocks):
            top = jnp.maximum(top, parts[h, b][2])
        acc = 0.0
        total = 0.0
        for b in range(blocks):
            o, l, t = parts[h, b]
            scale = jnp.exp2(t - top)
            acc = acc + o * scale
            total = total + l * scale
        results.append((acc / total, top + jnp.log2(total)))
    return results


def lane_eye(n):
    return lax.broadcasted_iota(jnp.int32, (n, n), 0) == lax.broadcasted_iota(jnp.int32, (n, n), 1)


def other_kernel(q_ref, *refs, c, kv_heads, pieces):
    kv_refs, msg_ref = refs[:-1], refs[-1]
    heads_q = split_heads(q_ref, kv_heads)
    m, d = heads_q[0].shape
    eye = lane_eye(d)
    packed = []
    for h, (o, lse) in enumerate(attend_blocks(heads_q, kv_refs, c)):
        msg_ref[h * m : (h + 1) * m, :] = o.astype(BF16)
        packed.append(jnp.sum(jnp.where(eye, lse.reshape(m // d, d, d), 0.0), axis=1))
    rest = jnp.concatenate(packed, axis=0)
    out = []
    for _ in range(3):
        piece = rest.astype(BF16).astype(F32)
        out.append(piece)
        rest = rest - piece
    used = 3 * out[0].shape[0]
    if pieces > used:
        out.append(jnp.zeros((pieces - used, d), F32))
    msg_ref[kv_heads * m :, :] = jnp.concatenate(out, axis=0).astype(BF16)


def own_kernel(q_ref, *refs, c, kv_heads):
    kv_refs, o_ref, lse_ref = refs[:-2], refs[-2], refs[-1]
    heads_q = split_heads(q_ref, kv_heads)
    for h, (o, lse) in enumerate(attend_blocks(heads_q, kv_refs, c)):
        o_ref[h] = o
        lse_ref[h] = lse


def suffix_kernel(
    len_ref, q_ref, k_ref, v_ref, op_ref, lp_ref, o_ref, lse_ref, item_ref, oi_ref, li_ref, *, c, kv_heads, batch, chunk
):
    rows, heads, d = q_ref.shape
    group = heads // kv_heads
    width = chunk * kv_heads
    chunks = k_ref.shape[1] // width
    lane = lax.broadcasted_iota(jnp.int32, (heads, width), 1)
    head = lax.broadcasted_iota(jnp.int32, (heads, width), 0) // group
    place = jnp.where(lane % kv_heads == head, lane // kv_heads, chunk * chunks)

    def enlist(r, count):
        for j in range(chunks):
            item_ref[count + j] = r * chunks + j
        return count + (len_ref[r] + chunk - 1) // chunk

    count = lax.fori_loop(0, rows, enlist, 0)
    for j in range(2 * batch):
        item_ref[count + j] = 0
    batches = (count + batch - 1) // batch

    def part(slot):
        r = slot // chunks
        j = slot - r * chunks
        return r, j, pl.ds(pl.multiple_of(j * width, width), width)

    def score_batch(i):
        found = []
        for t in range(batch):
            r, _, span = part(item_ref[i * batch + t])
            found.append(scores_of(q_ref[r], k_ref[r, span, :]))
        return tuple(found)

    def body(i, scores):
        ahead = score_batch(i + 1)
        weights = []
        for t in range(batch):
            r, j, _ = part(item_ref[i * batch + t])
            s = jnp.where(place < len_ref[r] - j * chunk, scores[t], -jnp.inf)
            top = jnp.max(s, axis=1, keepdims=True)
            w = jnp.exp2(s * c - top * c).astype(BF16)
            weights.append((w, top * c, jnp.sum(w.astype(F32), axis=1, keepdims=True)))
        for t in range(batch):
            slot = item_ref[i * batch + t]
            r, _, span = part(slot)
            w, top, total = weights[t]
            o = jnp.dot(w, v_ref[r, span, :], preferred_element_type=F32)
            oi_ref[slot] = o * (1.0 / total)
            li_ref[slot] = jnp.broadcast_to(top + jnp.log2(total), (heads, d))
        return ahead

    lax.fori_loop(0, batches, body, score_batch(0))

    def merge(r, _):
        live = (len_ref[r] + chunk - 1) // chunk
        rows_of = pl.ds(pl.multiple_of(r * group, group), group)
        parts = [
            (
                jnp.concatenate([op_ref[h, rows_of, :] for h in range(kv_heads)], axis=0),
                jnp.concatenate([lp_ref[h, rows_of, :] for h in range(kv_heads)], axis=0),
            )
        ]
        for j in range(chunks):
            slot = r * chunks + j
            parts.append((jnp.where(j < live, oi_ref[slot], 0.0), jnp.where(j < live, li_ref[slot], -jnp.inf)))
        top = parts[0][1]
        for p in parts[1:]:
            top = jnp.maximum(top, p[1])
        acc = 0.0
        total = 0.0
        for o, l in parts:
            w = jnp.exp2(l - top)
            acc = acc + o * w
            total = total + w
        o_ref[r] = acc / total
        lse_ref[r] = top + jnp.log2(total)
        return 0

    lax.fori_loop(0, rows, merge, 0, unroll=4 if rows % 4 == 0 else 1)


def merge_kernel(os_ref, ls_ref, *refs, kv_heads, group):
    msg_refs, out_ref = refs[:-1], refs[-1]
    rows, heads, d = os_ref.shape
    m = rows * group
    n = m // d
    eye = lane_eye(d)
    results = []
    for h in range(kv_heads):
        cols = slice(h * group, (h + 1) * group)
        parts = [(os_ref[:, cols, :].reshape(m, d), ls_ref[:, cols, :].reshape(m, d))]
        for msg in msg_refs:
            o = msg[h * m : (h + 1) * m, :].astype(F32)
            tail = msg[kv_heads * m :, :].astype(F32)
            lse = sum(tail[(p * kv_heads + h) * n : (p * kv_heads + h + 1) * n] for p in range(3))
            lse = jnp.where(eye, jnp.broadcast_to(lse[:, None, :], (n, d, d)), 0.0)
            lse = jnp.sum(lse, axis=2, keepdims=True).reshape(m, 1)
            parts.append((o, jnp.broadcast_to(lse, (m, d))))
        top = parts[0][1]
        for part in parts[1:]:
            top = jnp.maximum(top, part[1])
        acc = 0.0
        total = 0.0
        for o, l in parts:
            w = jnp.exp2(l - top)
            acc = acc + o * w
            total = total + w
        results.append((acc / total).reshape(rows, group, d))
    out_ref[...] = jnp.concatenate(results, axis=1).astype(BF16)


def shards(queries, prefix_keys, prefix_values, suffix_keys, suffix_values, lengths):
    rows, heads, d = queries.shape
    kv_heads = prefix_keys.shape[1]
    group = heads // kv_heads
    span = suffix_keys.shape[1]
    c = d ** (-0.5) * LOG2E
    n = lax.axis_size("ctx")
    cores = 2 if n % 2 == 0 else 1
    chips = n // cores
    m = rows * group
    pieces = -(-3 * kv_heads * (m // d) // 16) * 16

    def shift(x, by):
        return lax.ppermute(x, "ctx", [(i, (i + by) % n) for i in range(n)])

    def call(kernel, out_shape, operands, specs, scratch=(), mib=40, name=None, flops=0, moved=0):
        single = not isinstance(out_shape, tuple)
        return pl.pallas_call(
            kernel,
            out_shape=out_shape,
            in_specs=specs,
            out_specs=VMEM if single else (VMEM,) * len(out_shape),
            scratch_shapes=scratch,
            compiler_params=pltpu.CompilerParams(vmem_limit_bytes=mib << 20),
            cost_estimate=pl.CostEstimate(flops=flops, bytes_accessed=moved, transcendentals=0),
            name=name,
        )(*operands)

    flat = [prefix_keys.reshape(-1, d), prefix_values.reshape(-1, d)]
    if cores == 2:
        swap = [(i, i ^ 1) for i in range(n)]
        flat += [lax.ppermute(x, "ctx", swap) for x in flat]
    visiting = [shift(queries, j * cores) for j in range(1, chips)]

    flat = [x.reshape(-1, kv_heads, d).transpose(1, 0, 2) for x in flat]
    positions = cores * prefix_keys.shape[0]
    flops = 16 * m * kv_heads * positions * d
    moved = 4 * kv_heads * positions * d
    own_o, own_l = call(
        partial(own_kernel, c=c, kv_heads=kv_heads),
        (jax.ShapeDtypeStruct((kv_heads, m, d), F32),) * 2,
        (queries, *flat),
        [VMEM] * (1 + len(flat)),
        mib=24,
        name="own",
        flops=flops,
        moved=moved,
    )
    visiting, own_o, own_l = lax.optimization_barrier((visiting, own_o, own_l))
    message = jax.ShapeDtypeStruct((kv_heads * m + pieces, d), BF16)
    returned = []
    for j, q in enumerate(visiting):
        msg = call(
            partial(other_kernel, c=c, kv_heads=kv_heads, pieces=pieces),
            message,
            (q, *flat),
            [VMEM] * (1 + len(flat)),
            mib=24,
            name="visiting",
            flops=flops,
            moved=moved,
        )
        returned.append(shift(msg, -(j + 1) * cores))
    slots = span * kv_heads
    chunk = 128 if span % 128 == 0 else span
    batch = 8
    items = rows * (span // chunk)
    local = call(
        partial(suffix_kernel, c=c, kv_heads=kv_heads, batch=batch, chunk=chunk),
        (jax.ShapeDtypeStruct((rows, heads, d), F32),) * 2,
        (lengths, queries, suffix_keys.reshape(rows, slots, d), suffix_values.reshape(rows, slots, d), own_o, own_l),
        [pl.BlockSpec(memory_space=pltpu.SMEM)] + [VMEM] * 5,
        scratch=[
            pltpu.SMEM((items + 3 * batch,), jnp.int32),
            pltpu.VMEM((items, heads, d), F32),
            pltpu.VMEM((items, heads, d), F32),
        ],
        mib=12,
        name="suffix",
        flops=4 * rows * heads * slots * d,
        moved=4 * rows * slots * d,
    )
    operands = (*local, *returned)
    return call(
        partial(merge_kernel, kv_heads=kv_heads, group=group),
        jax.ShapeDtypeStruct((rows, heads, d), BF16),
        operands,
        [VMEM] * len(operands),
        mib=16,
        name="merge",
    )


def solution(mesh):
    placed = (
        P(("groups", "ctx"), "head", None),
        P(("groups", "ctx"), "head", None),
        P(("groups", "ctx"), "head", None),
        P(("groups", "ctx"), None, "head", None),
        P(("groups", "ctx"), None, "head", None),
        P(("groups", "ctx")),
    )
    return jax.shard_map(
        shards,
        mesh=mesh,
        in_specs=placed,
        out_specs=P(("groups", "ctx"), "head", None),
        check_vma=False,
    )
```

```python
from functools import partial

import jax
import jax.numpy as jnp
from jax import lax
from jax.experimental import pallas as pl
from jax.experimental.pallas import tpu as pltpu
from jax.sharding import PartitionSpec as P

LOG2E = 1.4426950408889634
F32 = jnp.float32
BF16 = jnp.bfloat16
VMEM = pl.BlockSpec(memory_space=pltpu.VMEM)


def split_heads(q_ref, kv_heads):
    rows, heads, d = q_ref.shape
    group = heads // kv_heads
    wide = q_ref[...].astype(F32)
    return [
        wide[:, h * group : (h + 1) * group, :].reshape(rows * group, d).astype(BF16)
        for h in range(kv_heads)
    ]


def scores_of(q, k):
    return lax.dot_general(q, k, (((1,), (1,)), ((), ())), preferred_element_type=F32)


def attend_blocks(heads_q, kv_refs, c):
    d = heads_q[0].shape[1]
    blocks = len(kv_refs) // 2
    items = [(h, b) for b in range(blocks) for h in range(len(heads_q))]
    parts = {}
    s = w = None
    for step in range(len(items) + 2):
        s_next = w_next = None
        if step < len(items):
            h, b = items[step]
            s_next = scores_of(heads_q[h], kv_refs[2 * b][h])
        if w is not None:
            h, b = items[step - 2]
            v = kv_refs[2 * b + 1][h]
            oa = jnp.dot(w[0], jnp.concatenate([v, jnp.ones_like(v)], axis=1), preferred_element_type=F32)
            parts[h, b] = (oa[:, :d], oa[:, d:], w[1])
        if s is not None:
            top = jnp.max(s, axis=1, keepdims=True)
            w_next = (jnp.exp2(s * c - top * c).astype(BF16), top * c)
        s, w = s_next, w_next
    results = []
    for h in range(len(heads_q)):
        top = parts[h, 0][2]
        for b in range(1, blocks):
            top = jnp.maximum(top, parts[h, b][2])
        acc = 0.0
        total = 0.0
        for b in range(blocks):
            o, l, t = parts[h, b]
            scale = jnp.exp2(t - top)
            acc = acc + o * scale
            total = total + l * scale
        results.append((acc / total, top + jnp.log2(total)))
    return results


def lane_eye(n):
    return lax.broadcasted_iota(jnp.int32, (n, n), 0) == lax.broadcasted_iota(jnp.int32, (n, n), 1)


def other_kernel(q_ref, *refs, c, kv_heads, pieces):
    kv_refs, msg_ref = refs[:-1], refs[-1]
    heads_q = split_heads(q_ref, kv_heads)
    m, d = heads_q[0].shape
    eye = lane_eye(d)
    packed = []
    for h, (o, lse) in enumerate(attend_blocks(heads_q, kv_refs, c)):
        msg_ref[h * m : (h + 1) * m, :] = o.astype(BF16)
        packed.append(jnp.sum(jnp.where(eye, lse.reshape(m // d, d, d), 0.0), axis=1))
    rest = jnp.concatenate(packed, axis=0)
    out = []
    for _ in range(3):
        piece = rest.astype(BF16).astype(F32)
        out.append(piece)
        rest = rest - piece
    used = 3 * out[0].shape[0]
    if pieces > used:
        out.append(jnp.zeros((pieces - used, d), F32))
    msg_ref[kv_heads * m :, :] = jnp.concatenate(out, axis=0).astype(BF16)


def own_kernel(q_hbm, k_hbm, v_hbm, *refs, c, kv_heads, given):
    others, refs = refs[:given], refs[given:]
    o_ref, lse_ref, kt_ref, vt_ref, q_ref, k_raw, v_raw, wide_k, wide_v, sems = refs
    copies = [
        pltpu.make_async_copy(src, dst, sems.at[i])
        for i, (src, dst) in enumerate(((q_hbm, q_ref), (k_hbm, k_raw), (v_hbm, v_raw)))
    ]
    for copy in copies:
        copy.start()
    for copy in copies:
        copy.wait()
    heads_q = split_heads(q_ref, kv_heads)
    positions = kt_ref.shape[1]
    for raw, wide, split in ((k_raw, wide_k, kt_ref), (v_raw, wide_v, vt_ref)):
        wide[...] = raw[...].astype(F32)
        for h in range(kv_heads):
            split[h] = wide[pl.ds(h, positions, stride=kv_heads), :].astype(BF16)
    for h, (o, lse) in enumerate(attend_blocks(heads_q, (*others, kt_ref, vt_ref), c)):
        o_ref[h] = o
        lse_ref[h] = lse


def suffix_kernel(
    len_ref, q_ref, k_ref, v_ref, op_ref, lp_ref, o_ref, lse_ref, item_ref, oi_ref, li_ref, *, c, kv_heads, batch, chunk
):
    rows, heads, d = q_ref.shape
    group = heads // kv_heads
    width = chunk * kv_heads
    chunks = k_ref.shape[1] // width
    lane = lax.broadcasted_iota(jnp.int32, (heads, width), 1)
    head = lax.broadcasted_iota(jnp.int32, (heads, width), 0) // group
    place = jnp.where(lane % kv_heads == head, lane // kv_heads, chunk * chunks)

    def enlist(r, count):
        for j in range(chunks):
            item_ref[count + j] = r * chunks + j
        return count + (len_ref[r] + chunk - 1) // chunk

    count = lax.fori_loop(0, rows, enlist, 0)
    for j in range(2 * batch):
        item_ref[count + j] = 0
    batches = (count + batch - 1) // batch

    def part(slot):
        r = slot // chunks
        j = slot - r * chunks
        return r, j, pl.ds(pl.multiple_of(j * width, width), width)

    def score_batch(i):
        found = []
        for t in range(batch):
            r, _, span = part(item_ref[i * batch + t])
            found.append(scores_of(q_ref[r], k_ref[r, span, :]))
        return tuple(found)

    def body(i, scores):
        ahead = score_batch(i + 1)
        weights = []
        for t in range(batch):
            r, j, _ = part(item_ref[i * batch + t])
            s = jnp.where(place < len_ref[r] - j * chunk, scores[t], -jnp.inf)
            top = jnp.max(s, axis=1, keepdims=True)
            w = jnp.exp2(s * c - top * c).astype(BF16)
            weights.append((w, top * c, jnp.sum(w.astype(F32), axis=1, keepdims=True)))
        for t in range(batch):
            slot = item_ref[i * batch + t]
            r, _, span = part(slot)
            w, top, total = weights[t]
            o = jnp.dot(w, v_ref[r, span, :], preferred_element_type=F32)
            oi_ref[slot] = o * (1.0 / total)
            li_ref[slot] = jnp.broadcast_to(top + jnp.log2(total), (heads, d))
        return ahead

    lax.fori_loop(0, batches, body, score_batch(0))

    def merge(r, _):
        live = (len_ref[r] + chunk - 1) // chunk
        rows_of = pl.ds(pl.multiple_of(r * group, group), group)
        parts = [
            (
                jnp.concatenate([op_ref[h, rows_of, :] for h in range(kv_heads)], axis=0),
                jnp.concatenate([lp_ref[h, rows_of, :] for h in range(kv_heads)], axis=0),
            )
        ]
        for j in range(chunks):
            slot = r * chunks + j
            parts.append((jnp.where(j < live, oi_ref[slot], 0.0), jnp.where(j < live, li_ref[slot], -jnp.inf)))
        top = parts[0][1]
        for p in parts[1:]:
            top = jnp.maximum(top, p[1])
        acc = 0.0
        total = 0.0
        for o, l in parts:
            w = jnp.exp2(l - top)
            acc = acc + o * w
            total = total + w
        o_ref[r] = acc / total
        lse_ref[r] = top + jnp.log2(total)
        return 0

    lax.fori_loop(0, rows, merge, 0, unroll=16 if rows % 16 == 0 else 1)


def merge_kernel(os_ref, ls_ref, *refs, kv_heads, group):
    msg_refs, out_ref = refs[:-1], refs[-1]
    rows, heads, d = os_ref.shape
    m = rows * group
    n = m // d
    eye = lane_eye(d)
    results = []
    for h in range(kv_heads):
        cols = slice(h * group, (h + 1) * group)
        parts = [(os_ref[:, cols, :].reshape(m, d), ls_ref[:, cols, :].reshape(m, d))]
        for msg in msg_refs:
            o = msg[h * m : (h + 1) * m, :].astype(F32)
            tail = msg[kv_heads * m :, :].astype(F32)
            lse = sum(tail[(p * kv_heads + h) * n : (p * kv_heads + h + 1) * n] for p in range(3))
            lse = jnp.where(eye, jnp.broadcast_to(lse[:, None, :], (n, d, d)), 0.0)
            lse = jnp.sum(lse, axis=2, keepdims=True).reshape(m, 1)
            parts.append((o, jnp.broadcast_to(lse, (m, d))))
        top = parts[0][1]
        for part in parts[1:]:
            top = jnp.maximum(top, part[1])
        acc = 0.0
        total = 0.0
        for o, l in parts:
            w = jnp.exp2(l - top)
            acc = acc + o * w
            total = total + w
        results.append((acc / total).reshape(rows, group, d))
    out_ref[...] = jnp.concatenate(results, axis=1).astype(BF16)


def shards(queries, prefix_keys, prefix_values, suffix_keys, suffix_values, lengths):
    rows, heads, d = queries.shape
    kv_heads = prefix_keys.shape[1]
    group = heads // kv_heads
    span = suffix_keys.shape[1]
    c = d ** (-0.5) * LOG2E
    n = lax.axis_size("ctx")
    cores = 2 if n % 2 == 0 else 1
    chips = n // cores
    m = rows * group
    pieces = -(-3 * kv_heads * (m // d) // 16) * 16

    def shift(x, by):
        return lax.ppermute(x, "ctx", [(i, (i + by) % n) for i in range(n)])

    def call(kernel, out_shape, operands, specs, scratch=(), mib=40, name=None, flops=0, moved=0):
        single = not isinstance(out_shape, tuple)
        return pl.pallas_call(
            kernel,
            out_shape=out_shape,
            in_specs=specs,
            out_specs=VMEM if single else (VMEM,) * len(out_shape),
            scratch_shapes=scratch,
            compiler_params=pltpu.CompilerParams(vmem_limit_bytes=mib << 20),
            cost_estimate=pl.CostEstimate(flops=flops, bytes_accessed=moved, transcendentals=0),
            name=name,
        )(*operands)

    raw = [prefix_keys.reshape(-1, d), prefix_values.reshape(-1, d)]
    flat = []
    if cores == 2:
        swap = [(i, i ^ 1) for i in range(n)]
        flat = [lax.ppermute(x, "ctx", swap).reshape(-1, kv_heads, d).transpose(1, 0, 2) for x in raw]
    visiting = [shift(queries, j * cores) for j in range(1, chips)]

    spread = prefix_keys.shape[0]
    positions = cores * spread
    flops = 16 * m * kv_heads * positions * d
    moved = 4 * kv_heads * positions * d
    anywhere = pl.BlockSpec(memory_space=pltpu.HBM)
    own_o, own_l, *split = call(
        partial(own_kernel, c=c, kv_heads=kv_heads, given=len(flat)),
        (jax.ShapeDtypeStruct((kv_heads, m, d), F32),) * 2 + (jax.ShapeDtypeStruct((kv_heads, spread, d), BF16),) * 2,
        (*(pltpu.with_memory_space_constraint(x, pltpu.HBM) for x in (queries, *raw)), *flat),
        [anywhere] * 3 + [VMEM] * len(flat),
        scratch=[pltpu.VMEM((rows, heads, d), BF16)]
        + [pltpu.VMEM((spread * kv_heads, d), BF16)] * 2
        + [pltpu.VMEM((spread * kv_heads, d), F32)] * 2
        + [pltpu.SemaphoreType.DMA((3,))],
        mib=28,
        name="own",
        flops=flops,
        moved=moved,
    )
    flat = [*flat, *split]
    visiting, own_o, own_l = lax.optimization_barrier((visiting, own_o, own_l))
    message = jax.ShapeDtypeStruct((kv_heads * m + pieces, d), BF16)
    returned = []
    for j, q in enumerate(visiting):
        msg = call(
            partial(other_kernel, c=c, kv_heads=kv_heads, pieces=pieces),
            message,
            (q, *flat),
            [VMEM] * (1 + len(flat)),
            mib=24,
            name="visiting",
            flops=flops,
            moved=moved,
        )
        returned.append(shift(msg, -(j + 1) * cores))
    slots = span * kv_heads
    chunk = 128 if span % 128 == 0 else span
    batch = 16
    items = rows * (span // chunk)
    local = call(
        partial(suffix_kernel, c=c, kv_heads=kv_heads, batch=batch, chunk=chunk),
        (jax.ShapeDtypeStruct((rows, heads, d), F32),) * 2,
        (lengths, queries, suffix_keys.reshape(rows, slots, d), suffix_values.reshape(rows, slots, d), own_o, own_l),
        [pl.BlockSpec(memory_space=pltpu.SMEM)] + [VMEM] * 5,
        scratch=[
            pltpu.SMEM((items + 3 * batch,), jnp.int32),
            pltpu.VMEM((items, heads, d), F32),
            pltpu.VMEM((items, heads, d), F32),
        ],
        mib=12,
        name="suffix",
        flops=4 * rows * heads * slots * d,
        moved=4 * rows * slots * d,
    )
    operands = (*local, *returned)
    return call(
        partial(merge_kernel, kv_heads=kv_heads, group=group),
        jax.ShapeDtypeStruct((rows, heads, d), BF16),
        operands,
        [VMEM] * len(operands),
        mib=16,
        name="merge",
    )


def solution(mesh):
    placed = (
        P(("groups", "ctx"), "head", None),
        P(("groups", "ctx"), "head", None),
        P(("groups", "ctx"), "head", None),
        P(("groups", "ctx"), None, "head", None),
        P(("groups", "ctx"), None, "head", None),
        P(("groups", "ctx")),
    )
    return jax.shard_map(
        shards,
        mesh=mesh,
        in_specs=placed,
        out_specs=P(("groups", "ctx"), "head", None),
        check_vma=False,
    )
```

```python
from functools import partial

import jax
import jax.numpy as jnp
from jax import lax
from jax.experimental import pallas as pl
from jax.experimental.pallas import tpu as pltpu
from jax.sharding import PartitionSpec as P

LOG2E = 1.4426950408889634
F32 = jnp.float32
BF16 = jnp.bfloat16
VMEM = pl.BlockSpec(memory_space=pltpu.VMEM)


def split_heads(q_ref, kv_heads):
    rows, heads, d = q_ref.shape
    group = heads // kv_heads
    wide = q_ref[...].astype(F32)
    return [
        wide[:, h * group : (h + 1) * group, :].reshape(rows * group, d).astype(BF16)
        for h in range(kv_heads)
    ]


def scores_of(q, k):
    return lax.dot_general(q, k, (((1,), (1,)), ((), ())), preferred_element_type=F32)


def attend_blocks(heads_q, kv_refs, c):
    d = heads_q[0].shape[1]
    blocks = len(kv_refs) // 2
    items = [(h, b) for h in range(len(heads_q)) for b in range(blocks)]
    parts = {}
    s = w = None
    for step in range(len(items) + 2):
        s_next = w_next = None
        if step < len(items):
            h, b = items[step]
            s_next = scores_of(heads_q[h], kv_refs[2 * b][h])
        if w is not None:
            h, b = items[step - 2]
            v = kv_refs[2 * b + 1][h]
            oa = jnp.dot(w[0], jnp.concatenate([v, jnp.ones_like(v)], axis=1), preferred_element_type=F32)
            parts[h, b] = (oa[:, :d], oa[:, d:], w[1])
        if s is not None:
            top = jnp.max(s, axis=1, keepdims=True)
            w_next = (jnp.exp2(s * c - top * c).astype(BF16), top * c)
        s, w = s_next, w_next
    results = []
    for h in range(len(heads_q)):
        top = parts[h, 0][2]
        for b in range(1, blocks):
            top = jnp.maximum(top, parts[h, b][2])
        acc = 0.0
        total = 0.0
        for b in range(blocks):
            o, l, t = parts[h, b]
            scale = jnp.exp2(t - top)
            acc = acc + o * scale
            total = total + l * scale
        results.append((acc / total, top + jnp.log2(total)))
    return results


def lane_eye(n):
    return lax.broadcasted_iota(jnp.int32, (n, n), 0) == lax.broadcasted_iota(jnp.int32, (n, n), 1)


def other_kernel(q_ref, *refs, c, kv_heads, pieces):
    kv_refs, msg_ref = refs[:-1], refs[-1]
    heads_q = split_heads(q_ref, kv_heads)
    m, d = heads_q[0].shape
    eye = lane_eye(d)
    packed = []
    for h, (o, lse) in enumerate(attend_blocks(heads_q, kv_refs, c)):
        msg_ref[h * m : (h + 1) * m, :] = o.astype(BF16)
        packed.append(jnp.sum(jnp.where(eye, lse.reshape(m // d, d, d), 0.0), axis=1))
    rest = jnp.concatenate(packed, axis=0)
    out = []
    for _ in range(3):
        piece = rest.astype(BF16).astype(F32)
        out.append(piece)
        rest = rest - piece
    used = 3 * out[0].shape[0]
    if pieces > used:
        out.append(jnp.zeros((pieces - used, d), F32))
    msg_ref[kv_heads * m :, :] = jnp.concatenate(out, axis=0).astype(BF16)


def own_kernel(q_ref, *refs, c, kv_heads, blocks):
    kv_refs, before, (o_ref, lse_ref) = refs[: 2 * blocks], refs[2 * blocks : -2], refs[-2:]
    heads_q = [q_ref[h] for h in range(kv_heads)]
    for h, (o, lse) in enumerate(attend_blocks(heads_q, kv_refs, c)):
        if before:
            o_old, lse_old = before[0][h], before[1][h]
            top = jnp.maximum(lse, lse_old)
            new, old = jnp.exp2(lse - top), jnp.exp2(lse_old - top)
            total = new + old
            o = (o * new + o_old * old) / total
            lse = top + jnp.log2(total)
        o_ref[h] = o
        lse_ref[h] = jnp.broadcast_to(lse, o.shape)


def suffix_kernel(
    len_ref, q_ref, k_ref, v_ref, op_ref, lp_ref, o_ref, lse_ref, item_ref, oi_ref, li_ref, *, c, kv_heads, batch, chunk
):
    rows, heads, d = q_ref.shape
    group = heads // kv_heads
    width = chunk * kv_heads
    chunks = k_ref.shape[1] // width
    lane = lax.broadcasted_iota(jnp.int32, (heads, width), 1)
    head = lax.broadcasted_iota(jnp.int32, (heads, width), 0) // group
    place = jnp.where(lane % kv_heads == head, lane // kv_heads, chunk * chunks)

    def enlist(r, count):
        for j in range(chunks):
            item_ref[count + j] = r * chunks + j
        return count + (len_ref[r] + chunk - 1) // chunk

    count = lax.fori_loop(0, rows, enlist, 0)
    for j in range(2 * batch):
        item_ref[count + j] = 0
    batches = (count + batch - 1) // batch

    def part(slot):
        r = slot // chunks
        j = slot - r * chunks
        return r, j, pl.ds(pl.multiple_of(j * width, width), width)

    def score_batch(i):
        found = []
        for t in range(batch):
            r, _, span = part(item_ref[i * batch + t])
            found.append(scores_of(q_ref[r], k_ref[r, span, :]))
        return tuple(found)

    def body(i, scores):
        ahead = score_batch(i + 1)
        weights = []
        for t in range(batch):
            r, j, _ = part(item_ref[i * batch + t])
            s = jnp.where(place < len_ref[r] - j * chunk, scores[t], -jnp.inf)
            top = jnp.max(s, axis=1, keepdims=True)
            w = jnp.exp2(s * c - top * c).astype(BF16)
            weights.append((w, top * c, jnp.sum(w.astype(F32), axis=1, keepdims=True)))
        for t in range(batch):
            slot = item_ref[i * batch + t]
            r, _, span = part(slot)
            w, top, total = weights[t]
            o = jnp.dot(w, v_ref[r, span, :], preferred_element_type=F32)
            oi_ref[slot] = o * (1.0 / total)
            li_ref[slot] = jnp.broadcast_to(top + jnp.log2(total), (heads, d))
        return ahead

    lax.fori_loop(0, batches, body, score_batch(0))

    def merge(r, _):
        live = (len_ref[r] + chunk - 1) // chunk
        rows_of = pl.ds(pl.multiple_of(r * group, group), group)
        parts = [
            (
                jnp.concatenate([op_ref[h, rows_of, :] for h in range(kv_heads)], axis=0),
                jnp.concatenate([lp_ref[h, rows_of, :] for h in range(kv_heads)], axis=0),
            )
        ]
        for j in range(chunks):
            slot = r * chunks + j
            parts.append((jnp.where(j < live, oi_ref[slot], 0.0), jnp.where(j < live, li_ref[slot], -jnp.inf)))
        top = parts[0][1]
        for p in parts[1:]:
            top = jnp.maximum(top, p[1])
        acc = 0.0
        total = 0.0
        for o, l in parts:
            w = jnp.exp2(l - top)
            acc = acc + o * w
            total = total + w
        o_ref[r] = acc / total
        lse_ref[r] = top + jnp.log2(total)
        return 0

    lax.fori_loop(0, rows, merge, 0, unroll=16 if rows % 16 == 0 else 1)


def merge_kernel(os_ref, ls_ref, *refs, kv_heads, group):
    msg_refs, out_ref = refs[:-1], refs[-1]
    rows, heads, d = os_ref.shape
    m = rows * group
    n = m // d
    eye = lane_eye(d)
    results = []
    for h in range(kv_heads):
        cols = slice(h * group, (h + 1) * group)
        parts = [(os_ref[:, cols, :].reshape(m, d), ls_ref[:, cols, :].reshape(m, d))]
        for msg in msg_refs:
            o = msg[h * m : (h + 1) * m, :].astype(F32)
            tail = msg[kv_heads * m :, :].astype(F32)
            lse = sum(tail[(p * kv_heads + h) * n : (p * kv_heads + h + 1) * n] for p in range(3))
            lse = jnp.where(eye, jnp.broadcast_to(lse[:, None, :], (n, d, d)), 0.0)
            lse = jnp.sum(lse, axis=2, keepdims=True).reshape(m, 1)
            parts.append((o, jnp.broadcast_to(lse, (m, d))))
        top = parts[0][1]
        for part in parts[1:]:
            top = jnp.maximum(top, part[1])
        acc = 0.0
        total = 0.0
        for o, l in parts:
            w = jnp.exp2(l - top)
            acc = acc + o * w
            total = total + w
        results.append((acc / total).reshape(rows, group, d))
    out_ref[...] = jnp.concatenate(results, axis=1).astype(BF16)


def shards(queries, prefix_keys, prefix_values, suffix_keys, suffix_values, lengths):
    rows, heads, d = queries.shape
    kv_heads = prefix_keys.shape[1]
    group = heads // kv_heads
    span = suffix_keys.shape[1]
    c = d ** (-0.5) * LOG2E
    n = lax.axis_size("ctx")
    cores = 2 if n % 2 == 0 else 1
    chips = n // cores
    m = rows * group
    pieces = -(-3 * kv_heads * (m // d) // 16) * 16

    def shift(x, by):
        return lax.ppermute(x, "ctx", [(i, (i + by) % n) for i in range(n)])

    def call(kernel, out_shape, operands, specs, scratch=(), mib=40, name=None, flops=0, moved=0):
        single = not isinstance(out_shape, tuple)
        return pl.pallas_call(
            kernel,
            out_shape=out_shape,
            in_specs=specs,
            out_specs=VMEM if single else (VMEM,) * len(out_shape),
            scratch_shapes=scratch,
            compiler_params=pltpu.CompilerParams(vmem_limit_bytes=mib << 20),
            cost_estimate=pl.CostEstimate(flops=flops, bytes_accessed=moved, transcendentals=0),
            name=name,
        )(*operands)

    raw = [prefix_keys.reshape(-1, d), prefix_values.reshape(-1, d)]
    split_queries = queries.reshape(rows, kv_heads, group, d).transpose(1, 0, 2, 3).reshape(kv_heads, m, d)

    def by_head(x):
        return x.reshape(-1, kv_heads, d).transpose(1, 0, 2)

    visiting = [shift(queries, j * cores) for j in range(1, chips)]

    spread = prefix_keys.shape[0]
    flops = 16 * m * kv_heads * spread * d
    moved = 4 * kv_heads * spread * d

    def own_rows(kv, before):
        operands = (split_queries, *kv, *before)
        return call(
            partial(own_kernel, c=c, kv_heads=kv_heads, blocks=len(kv) // 2),
            (jax.ShapeDtypeStruct((kv_heads, m, d), F32),) * 2,
            operands,
            [VMEM] * len(operands),
            mib=24,
            name="own",
            flops=flops,
            moved=moved,
        )

    flat = []
    own = ()
    if cores == 2:
        swap = [(i, i ^ 1) for i in range(n)]
        flat = [by_head(lax.ppermute(x, "ctx", swap)) for x in raw]
        own = own_rows(flat, ())
        raw, own = lax.optimization_barrier((raw, own))
    raw = [by_head(x) for x in raw]
    own_o, own_l = own_rows(raw, own)
    flat = [*flat, *raw]
    visiting, own_o, own_l = lax.optimization_barrier((visiting, own_o, own_l))
    message = jax.ShapeDtypeStruct((kv_heads * m + pieces, d), BF16)
    returned = []
    for j, q in enumerate(visiting):
        msg = call(
            partial(other_kernel, c=c, kv_heads=kv_heads, pieces=pieces),
            message,
            (q, *flat),
            [VMEM] * (1 + len(flat)),
            mib=24,
            name="visiting",
            flops=cores * flops,
            moved=cores * moved,
        )
        returned.append(shift(msg, -(j + 1) * cores))
    slots = span * kv_heads
    chunk = 128 if span % 128 == 0 else span
    batch = 16
    items = rows * (span // chunk)
    local = call(
        partial(suffix_kernel, c=c, kv_heads=kv_heads, batch=batch, chunk=chunk),
        (jax.ShapeDtypeStruct((rows, heads, d), F32),) * 2,
        (lengths, queries, suffix_keys.reshape(rows, slots, d), suffix_values.reshape(rows, slots, d), own_o, own_l),
        [pl.BlockSpec(memory_space=pltpu.SMEM)] + [VMEM] * 5,
        scratch=[
            pltpu.SMEM((items + 3 * batch,), jnp.int32),
            pltpu.VMEM((items, heads, d), F32),
            pltpu.VMEM((items, heads, d), F32),
        ],
        mib=12,
        name="suffix",
        flops=4 * rows * heads * slots * d,
        moved=4 * rows * slots * d,
    )
    operands = (*local, *returned)
    return call(
        partial(merge_kernel, kv_heads=kv_heads, group=group),
        jax.ShapeDtypeStruct((rows, heads, d), BF16),
        operands,
        [VMEM] * len(operands),
        mib=16,
        name="merge",
    )


def solution(mesh):
    placed = (
        P(("groups", "ctx"), "head", None),
        P(("groups", "ctx"), "head", None),
        P(("groups", "ctx"), "head", None),
        P(("groups", "ctx"), None, "head", None),
        P(("groups", "ctx"), None, "head", None),
        P(("groups", "ctx")),
    )
    return jax.shard_map(
        shards,
        mesh=mesh,
        in_specs=placed,
        out_specs=P(("groups", "ctx"), "head", None),
        check_vma=False,
    )
```

```python
from functools import partial

import jax
import jax.numpy as jnp
from jax import lax
from jax.experimental import pallas as pl
from jax.experimental.pallas import tpu as pltpu
from jax.sharding import PartitionSpec as P

LOG2E = 1.4426950408889634
F32 = jnp.float32
BF16 = jnp.bfloat16
VMEM = pl.BlockSpec(memory_space=pltpu.VMEM)


def split_heads(q_ref, kv_heads):
    rows, heads, d = q_ref.shape
    group = heads // kv_heads
    wide = q_ref[...].astype(F32)
    return [
        wide[:, h * group : (h + 1) * group, :].reshape(rows * group, d).astype(BF16)
        for h in range(kv_heads)
    ]


def scores_of(q, k):
    return lax.dot_general(q, k, (((1,), (1,)), ((), ())), preferred_element_type=F32)


def attend_blocks(heads_q, kv_refs, c):
    d = heads_q[0].shape[1]
    blocks = len(kv_refs) // 2
    items = [(h, b) for h in range(len(heads_q)) for b in range(blocks)]
    parts = {}
    s = w = None
    for step in range(len(items) + 2):
        s_next = w_next = None
        if step < len(items):
            h, b = items[step]
            s_next = scores_of(heads_q[h], kv_refs[2 * b][h])
        if w is not None:
            h, b = items[step - 2]
            v = kv_refs[2 * b + 1][h]
            oa = jnp.dot(w[0], jnp.concatenate([v, jnp.ones_like(v)], axis=1), preferred_element_type=F32)
            parts[h, b] = (oa[:, :d], oa[:, d:], w[1])
        if s is not None:
            top = jnp.max(s, axis=1, keepdims=True)
            w_next = (jnp.exp2(s * c - top * c).astype(BF16), top * c)
        s, w = s_next, w_next
    results = []
    for h in range(len(heads_q)):
        top = parts[h, 0][2]
        for b in range(1, blocks):
            top = jnp.maximum(top, parts[h, b][2])
        acc = 0.0
        total = 0.0
        for b in range(blocks):
            o, l, t = parts[h, b]
            scale = jnp.exp2(t - top)
            acc = acc + o * scale
            total = total + l * scale
        results.append((acc / total, top + jnp.log2(total)))
    return results


def lane_eye(n):
    return lax.broadcasted_iota(jnp.int32, (n, n), 0) == lax.broadcasted_iota(jnp.int32, (n, n), 1)


def other_kernel(q_ref, *refs, c, kv_heads, pieces):
    kv_refs, msg_ref = refs[:-1], refs[-1]
    heads_q = split_heads(q_ref, kv_heads)
    m, d = heads_q[0].shape
    eye = lane_eye(d)
    packed = []
    for h, (o, lse) in enumerate(attend_blocks(heads_q, kv_refs, c)):
        msg_ref[h * m : (h + 1) * m, :] = o.astype(BF16)
        packed.append(jnp.sum(jnp.where(eye, lse.reshape(m // d, d, d), 0.0), axis=1))
    rest = jnp.concatenate(packed, axis=0)
    out = []
    for _ in range(3):
        piece = rest.astype(BF16).astype(F32)
        out.append(piece)
        rest = rest - piece
    used = 3 * out[0].shape[0]
    if pieces > used:
        out.append(jnp.zeros((pieces - used, d), F32))
    msg_ref[kv_heads * m :, :] = jnp.concatenate(out, axis=0).astype(BF16)


def own_kernel(q_ref, *refs, c, kv_heads, blocks):
    kv_refs, before, (o_ref, lse_ref) = refs[: 2 * blocks], refs[2 * blocks : -2], refs[-2:]
    heads_q = [q_ref[h] for h in range(kv_heads)]
    for h, (o, lse) in enumerate(attend_blocks(heads_q, kv_refs, c)):
        if before:
            o_old, lse_old = before[0][h], before[1][h]
            top = jnp.maximum(lse, lse_old)
            new, old = jnp.exp2(lse - top), jnp.exp2(lse_old - top)
            total = new + old
            o = (o * new + o_old * old) / total
            lse = top + jnp.log2(total)
        o_ref[h] = o
        lse_ref[h] = jnp.broadcast_to(lse, o.shape)


def queries_kernel(len_ref, q_hbm, o_ref, item_ref, q_ref, sem, *, kv_heads, chunk, chunks, pad):
    copy = pltpu.make_async_copy(q_hbm, q_ref, sem)
    copy.start()
    rows = q_ref.shape[0]

    def enlist(r, count):
        for j in range(chunks):
            item_ref[count + j] = r * chunks + j
        return count + (len_ref[r] + chunk - 1) // chunk

    count = lax.fori_loop(0, rows, enlist, 0, unroll=16 if rows % 16 == 0 else 1)
    for j in range(pad):
        item_ref[count + j] = 0
    item_ref[rows * chunks + pad] = count
    copy.wait()
    for h, q in enumerate(split_heads(q_ref, kv_heads)):
        o_ref[h] = q


def suffix_kernel(
    len_ref, item_ref, q_ref, k_ref, v_ref, op_ref, lp_ref, o_ref, lse_ref, oi_ref, li_ref, *, c, kv_heads, batch, chunk
):
    rows, heads, d = q_ref.shape
    group = heads // kv_heads
    width = chunk * kv_heads
    chunks = k_ref.shape[1] // width
    lane = lax.broadcasted_iota(jnp.int32, (heads, width), 1)
    head = lax.broadcasted_iota(jnp.int32, (heads, width), 0) // group
    place = jnp.where(lane % kv_heads == head, lane // kv_heads, chunk * chunks)

    count = item_ref[rows * chunks + 2 * batch]
    batches = (count + batch - 1) // batch

    def part(slot):
        r = slot // chunks
        j = slot - r * chunks
        return r, j, pl.ds(pl.multiple_of(j * width, width), width)

    def score_batch(i):
        found = []
        for t in range(batch):
            r, _, span = part(item_ref[i * batch + t])
            found.append(scores_of(q_ref[r], k_ref[r, span, :]))
        return tuple(found)

    def body(i, scores):
        ahead = score_batch(i + 1)
        weights = []
        for t in range(batch):
            r, j, _ = part(item_ref[i * batch + t])
            s = jnp.where(place < len_ref[r] - j * chunk, scores[t], -jnp.inf)
            top = jnp.max(s, axis=1, keepdims=True)
            w = jnp.exp2(s * c - top * c).astype(BF16)
            weights.append((w, top * c, jnp.sum(w.astype(F32), axis=1, keepdims=True)))
        for t in range(batch):
            slot = item_ref[i * batch + t]
            r, _, span = part(slot)
            w, top, total = weights[t]
            o = jnp.dot(w, v_ref[r, span, :], preferred_element_type=F32)
            oi_ref[slot] = o * (1.0 / total)
            li_ref[slot] = jnp.broadcast_to(top + jnp.log2(total), (heads, d))
        return ahead

    lax.fori_loop(0, batches, body, score_batch(0))

    def merge(r, _):
        live = (len_ref[r] + chunk - 1) // chunk
        rows_of = pl.ds(pl.multiple_of(r * group, group), group)
        parts = [
            (
                jnp.concatenate([op_ref[h, rows_of, :] for h in range(kv_heads)], axis=0),
                jnp.concatenate([lp_ref[h, rows_of, :] for h in range(kv_heads)], axis=0),
            )
        ]
        for j in range(chunks):
            slot = r * chunks + j
            parts.append((jnp.where(j < live, oi_ref[slot], 0.0), jnp.where(j < live, li_ref[slot], -jnp.inf)))
        top = parts[0][1]
        for p in parts[1:]:
            top = jnp.maximum(top, p[1])
        acc = 0.0
        total = 0.0
        for o, l in parts:
            w = jnp.exp2(l - top)
            acc = acc + o * w
            total = total + w
        o_ref[r] = acc / total
        lse_ref[r] = top + jnp.log2(total)
        return 0

    lax.fori_loop(0, rows, merge, 0, unroll=16 if rows % 16 == 0 else 1)


def merge_kernel(os_ref, ls_ref, *refs, kv_heads, group):
    msg_refs, out_ref = refs[:-1], refs[-1]
    rows, heads, d = os_ref.shape
    m = rows * group
    n = m // d
    eye = lane_eye(d)
    results = []
    for h in range(kv_heads):
        cols = slice(h * group, (h + 1) * group)
        parts = [(os_ref[:, cols, :].reshape(m, d), ls_ref[:, cols, :].reshape(m, d))]
        for msg in msg_refs:
            o = msg[h * m : (h + 1) * m, :].astype(F32)
            tail = msg[kv_heads * m :, :].astype(F32)
            lse = sum(tail[(p * kv_heads + h) * n : (p * kv_heads + h + 1) * n] for p in range(3))
            lse = jnp.where(eye, jnp.broadcast_to(lse[:, None, :], (n, d, d)), 0.0)
            lse = jnp.sum(lse, axis=2, keepdims=True).reshape(m, 1)
            parts.append((o, jnp.broadcast_to(lse, (m, d))))
        top = parts[0][1]
        for part in parts[1:]:
            top = jnp.maximum(top, part[1])
        acc = 0.0
        total = 0.0
        for o, l in parts:
            w = jnp.exp2(l - top)
            acc = acc + o * w
            total = total + w
        results.append((acc / total).reshape(rows, group, d))
    out_ref[...] = jnp.concatenate(results, axis=1).astype(BF16)


def shards(queries, prefix_keys, prefix_values, suffix_keys, suffix_values, lengths):
    rows, heads, d = queries.shape
    kv_heads = prefix_keys.shape[1]
    group = heads // kv_heads
    span = suffix_keys.shape[1]
    c = d ** (-0.5) * LOG2E
    n = lax.axis_size("ctx")
    cores = 2 if n % 2 == 0 else 1
    chips = n // cores
    m = rows * group
    pieces = -(-3 * kv_heads * (m // d) // 16) * 16

    def shift(x, by):
        return lax.ppermute(x, "ctx", [(i, (i + by) % n) for i in range(n)])

    def call(kernel, out_shape, operands, specs, scratch=(), outs=None, mib=40, name=None, flops=0, moved=0):
        single = not isinstance(out_shape, tuple)
        return pl.pallas_call(
            kernel,
            out_shape=out_shape,
            in_specs=specs,
            out_specs=outs or (VMEM if single else (VMEM,) * len(out_shape)),
            scratch_shapes=scratch,
            compiler_params=pltpu.CompilerParams(vmem_limit_bytes=mib << 20),
            cost_estimate=pl.CostEstimate(flops=flops, bytes_accessed=moved, transcendentals=0),
            name=name,
        )(*operands)

    raw = [prefix_keys.reshape(-1, d), prefix_values.reshape(-1, d)]
    slots = span * kv_heads
    chunk = 128 if span % 128 == 0 else span
    batch = 16
    items = rows * (span // chunk)
    smem = pl.BlockSpec(memory_space=pltpu.SMEM)
    split_queries, table = call(
        partial(queries_kernel, kv_heads=kv_heads, chunk=chunk, chunks=span // chunk, pad=2 * batch),
        (jax.ShapeDtypeStruct((kv_heads, m, d), BF16), jax.ShapeDtypeStruct((items + 2 * batch + 1,), jnp.int32)),
        (lengths, pltpu.with_memory_space_constraint(queries, pltpu.HBM)),
        [smem, pl.BlockSpec(memory_space=pltpu.HBM)],
        scratch=[pltpu.VMEM((rows, heads, d), BF16), pltpu.SemaphoreType.DMA],
        outs=(VMEM, smem),
        mib=16,
        name="queries",
        moved=4 * m * kv_heads * d,
    )

    def by_head(x):
        return x.reshape(-1, kv_heads, d).transpose(1, 0, 2)

    visiting = [shift(queries, j * cores) for j in range(1, chips)]

    spread = prefix_keys.shape[0]
    flops = 16 * m * kv_heads * spread * d
    moved = 4 * kv_heads * spread * d

    def own_rows(kv, before):
        operands = (split_queries, *kv, *before)
        return call(
            partial(own_kernel, c=c, kv_heads=kv_heads, blocks=len(kv) // 2),
            (jax.ShapeDtypeStruct((kv_heads, m, d), F32),) * 2,
            operands,
            [VMEM] * len(operands),
            mib=24,
            name="own",
            flops=flops,
            moved=moved,
        )

    flat = []
    own = ()
    if cores == 2:
        swap = [(i, i ^ 1) for i in range(n)]
        flat = [by_head(lax.ppermute(x, "ctx", swap)) for x in raw]
        own = own_rows(flat, ())
        raw, own = lax.optimization_barrier((raw, own))
    raw = [by_head(x) for x in raw]
    own_o, own_l = own_rows(raw, own)
    flat = [*flat, *raw]
    visiting, own_o, own_l = lax.optimization_barrier((visiting, own_o, own_l))
    message = jax.ShapeDtypeStruct((kv_heads * m + pieces, d), BF16)
    returned = []
    for j, q in enumerate(visiting):
        msg = call(
            partial(other_kernel, c=c, kv_heads=kv_heads, pieces=pieces),
            message,
            (q, *flat),
            [VMEM] * (1 + len(flat)),
            mib=24,
            name="visiting",
            flops=cores * flops,
            moved=cores * moved,
        )
        returned.append(shift(msg, -(j + 1) * cores))
    local = call(
        partial(suffix_kernel, c=c, kv_heads=kv_heads, batch=batch, chunk=chunk),
        (jax.ShapeDtypeStruct((rows, heads, d), F32),) * 2,
        (lengths, table, queries, suffix_keys.reshape(rows, slots, d), suffix_values.reshape(rows, slots, d), own_o, own_l),
        [smem] * 2 + [VMEM] * 5,
        scratch=[
            pltpu.VMEM((items, heads, d), F32),
            pltpu.VMEM((items, heads, d), F32),
        ],
        mib=12,
        name="suffix",
        flops=4 * rows * heads * slots * d,
        moved=4 * rows * slots * d,
    )
    operands = (*local, *returned)
    return call(
        partial(merge_kernel, kv_heads=kv_heads, group=group),
        jax.ShapeDtypeStruct((rows, heads, d), BF16),
        operands,
        [VMEM] * len(operands),
        mib=16,
        name="merge",
    )


def solution(mesh):
    placed = (
        P(("groups", "ctx"), "head", None),
        P(("groups", "ctx"), "head", None),
        P(("groups", "ctx"), "head", None),
        P(("groups", "ctx"), None, "head", None),
        P(("groups", "ctx"), None, "head", None),
        P(("groups", "ctx")),
    )
    return jax.shard_map(
        shards,
        mesh=mesh,
        in_specs=placed,
        out_specs=P(("groups", "ctx"), "head", None),
        check_vma=False,
    )
```

```python
from functools import partial

import jax
import jax.numpy as jnp
from jax import lax
from jax.experimental import pallas as pl
from jax.experimental.pallas import tpu as pltpu
from jax.sharding import PartitionSpec as P

LOG2E = 1.4426950408889634
F32 = jnp.float32
BF16 = jnp.bfloat16
VMEM = pl.BlockSpec(memory_space=pltpu.VMEM)


def split_heads(q_ref, kv_heads):
    rows, heads, d = q_ref.shape
    group = heads // kv_heads
    wide = q_ref[...].astype(F32)
    return [
        wide[:, h * group : (h + 1) * group, :].reshape(rows * group, d).astype(BF16)
        for h in range(kv_heads)
    ]


def scores_of(q, k):
    return lax.dot_general(q, k, (((1,), (1,)), ((), ())), preferred_element_type=F32)


def attend_blocks(heads_q, kv_refs, c, ready=()):
    d = heads_q[0].shape[1]
    blocks = len(kv_refs) // 2
    items = [(h, b) for h in range(len(heads_q)) for b in range(blocks)]
    parts = {}
    ready = list(ready)
    s = w = None

    def weigh(w, top, v):
        oa = jnp.dot(w, jnp.concatenate([v, jnp.ones_like(v)], axis=1), preferred_element_type=F32)
        return oa[:, :d], oa[:, d:], top

    def take_ready():
        h, *rest = ready.pop(0)
        parts[h, blocks] = weigh(*rest)

    for step in range(len(items) + 2):
        s_next = w_next = None
        if step < len(items):
            h, b = items[step]
            s_next = scores_of(heads_q[h], kv_refs[2 * b][h])
        if w is not None:
            h, b = items[step - 2]
            parts[h, b] = weigh(*w, kv_refs[2 * b + 1][h])
        elif ready:
            take_ready()
        if s is not None:
            top = jnp.max(s, axis=1, keepdims=True)
            w_next = (jnp.exp2(s * c - top * c).astype(BF16), top * c)
        s, w = s_next, w_next
    while ready:
        take_ready()
    results = []
    for h in range(len(heads_q)):
        mine = [parts[h, b] for b in range(blocks + 1) if (h, b) in parts]
        top = mine[0][2]
        for part in mine[1:]:
            top = jnp.maximum(top, part[2])
        acc = 0.0
        total = 0.0
        for o, l, t in mine:
            scale = jnp.exp2(t - top)
            acc = acc + o * scale
            total = total + l * scale
        results.append((acc / total, top + jnp.log2(total)))
    return results


def lane_eye(n):
    return lax.broadcasted_iota(jnp.int32, (n, n), 0) == lax.broadcasted_iota(jnp.int32, (n, n), 1)


def other_kernel(q_ref, *refs, c, kv_heads, pieces):
    kv_refs, msg_ref = refs[:-1], refs[-1]
    heads_q = split_heads(q_ref, kv_heads)
    m, d = heads_q[0].shape
    eye = lane_eye(d)
    packed = []
    for h, (o, lse) in enumerate(attend_blocks(heads_q, kv_refs, c)):
        msg_ref[h * m : (h + 1) * m, :] = o.astype(BF16)
        packed.append(jnp.sum(jnp.where(eye, lse.reshape(m // d, d, d), 0.0), axis=1))
    rest = jnp.concatenate(packed, axis=0)
    out = []
    for _ in range(3):
        piece = rest.astype(BF16).astype(F32)
        out.append(piece)
        rest = rest - piece
    used = 3 * out[0].shape[0]
    if pieces > used:
        out.append(jnp.zeros((pieces - used, d), F32))
    msg_ref[kv_heads * m :, :] = jnp.concatenate(out, axis=0).astype(BF16)


def first_kernel(q_ref, k_ref, w_ref, top_ref, *, c, kv_heads):
    scores = [scores_of(q_ref[h], k_ref[h]) for h in range(kv_heads)]
    for h in range(kv_heads):
        top = jnp.max(scores[h], axis=1, keepdims=True)
        w_ref[h] = jnp.exp2(scores[h] * c - top * c).astype(BF16)
        top_ref[h] = jnp.broadcast_to(top * c, top_ref.shape[1:])


def own_kernel(q_ref, k_ref, v_ref, *refs, c, kv_heads):
    before, (o_ref, lse_ref) = refs[:-2], refs[-2:]
    heads_q = [q_ref[h] for h in range(kv_heads)]
    ready = ()
    if before:
        w_ref, top_ref, late_ref = before
        ready = [(h, w_ref[h], top_ref[h][:, :1], late_ref[h]) for h in range(kv_heads)]
    for h, (o, lse) in enumerate(attend_blocks(heads_q, (k_ref, v_ref), c, ready)):
        o_ref[h] = o
        lse_ref[h] = jnp.broadcast_to(lse, o.shape)


def queries_kernel(len_hbm, q_hbm, o_ref, item_ref, len_ref, q_ref, sems, *, kv_heads, chunk, chunks, pad):
    numbers = pltpu.make_async_copy(len_hbm, len_ref, sems.at[0])
    numbers.start()
    copy = pltpu.make_async_copy(q_hbm, q_ref, sems.at[1])
    copy.start()
    numbers.wait()
    rows = q_ref.shape[0]

    def enlist(r, count):
        for j in range(chunks):
            item_ref[count + j] = r * chunks + j
        return count + (len_ref[r] + chunk - 1) // chunk

    count = lax.fori_loop(0, rows, enlist, 0, unroll=16 if rows % 16 == 0 else 1)
    for j in range(pad):
        item_ref[count + j] = 0
    item_ref[rows * chunks + pad] = count
    copy.wait()
    for h, q in enumerate(split_heads(q_ref, kv_heads)):
        o_ref[h] = q


def suffix_kernel(
    len_ref, item_ref, q_ref, k_ref, v_ref, op_ref, lp_ref, o_ref, lse_ref, oi_ref, li_ref, *, c, kv_heads, batch, chunk
):
    rows, heads, d = q_ref.shape
    group = heads // kv_heads
    width = chunk * kv_heads
    chunks = k_ref.shape[1] // width
    lane = lax.broadcasted_iota(jnp.int32, (heads, width), 1)
    head = lax.broadcasted_iota(jnp.int32, (heads, width), 0) // group
    place = jnp.where(lane % kv_heads == head, lane // kv_heads, chunk * chunks)

    count = item_ref[rows * chunks + 2 * batch]
    batches = (count + batch - 1) // batch

    def part(slot):
        r = slot // chunks
        j = slot - r * chunks
        return r, j, pl.ds(pl.multiple_of(j * width, width), width)

    def score_batch(i):
        found = []
        for t in range(batch):
            r, _, span = part(item_ref[i * batch + t])
            found.append(scores_of(q_ref[r], k_ref[r, span, :]))
        return tuple(found)

    def body(i, scores):
        ahead = score_batch(i + 1)
        weights = []
        for t in range(batch):
            r, j, _ = part(item_ref[i * batch + t])
            s = jnp.where(place < len_ref[r] - j * chunk, scores[t], -jnp.inf)
            top = jnp.max(s, axis=1, keepdims=True)
            w = jnp.exp2(s * c - top * c).astype(BF16)
            weights.append((w, top * c, jnp.sum(w.astype(F32), axis=1, keepdims=True)))
        for t in range(batch):
            slot = item_ref[i * batch + t]
            r, _, span = part(slot)
            w, top, total = weights[t]
            o = jnp.dot(w, v_ref[r, span, :], preferred_element_type=F32)
            oi_ref[slot] = o * (1.0 / total)
            li_ref[slot] = jnp.broadcast_to(top + jnp.log2(total), (heads, d))
        return ahead

    lax.fori_loop(0, batches, body, score_batch(0))

    def merge(r, _):
        live = (len_ref[r] + chunk - 1) // chunk
        rows_of = pl.ds(pl.multiple_of(r * group, group), group)
        parts = [
            (
                jnp.concatenate([op_ref[h, rows_of, :] for h in range(kv_heads)], axis=0),
                jnp.concatenate([lp_ref[h, rows_of, :] for h in range(kv_heads)], axis=0),
            )
        ]
        for j in range(chunks):
            slot = r * chunks + j
            parts.append((jnp.where(j < live, oi_ref[slot], 0.0), jnp.where(j < live, li_ref[slot], -jnp.inf)))
        top = parts[0][1]
        for p in parts[1:]:
            top = jnp.maximum(top, p[1])
        acc = 0.0
        total = 0.0
        for o, l in parts:
            w = jnp.exp2(l - top)
            acc = acc + o * w
            total = total + w
        o_ref[r] = acc / total
        lse_ref[r] = top + jnp.log2(total)
        return 0

    lax.fori_loop(0, rows, merge, 0, unroll=16 if rows % 16 == 0 else 1)


def merge_kernel(os_ref, ls_ref, *refs, kv_heads, group):
    msg_refs, out_ref = refs[:-1], refs[-1]
    rows, heads, d = os_ref.shape
    m = rows * group
    n = m // d
    eye = lane_eye(d)
    results = []
    for h in range(kv_heads):
        cols = slice(h * group, (h + 1) * group)
        parts = [(os_ref[:, cols, :].reshape(m, d), ls_ref[:, cols, :].reshape(m, d))]
        for msg in msg_refs:
            o = msg[h * m : (h + 1) * m, :].astype(F32)
            tail = msg[kv_heads * m :, :].astype(F32)
            lse = sum(tail[(p * kv_heads + h) * n : (p * kv_heads + h + 1) * n] for p in range(3))
            lse = jnp.where(eye, jnp.broadcast_to(lse[:, None, :], (n, d, d)), 0.0)
            lse = jnp.sum(lse, axis=2, keepdims=True).reshape(m, 1)
            parts.append((o, jnp.broadcast_to(lse, (m, d))))
        top = parts[0][1]
        for part in parts[1:]:
            top = jnp.maximum(top, part[1])
        acc = 0.0
        total = 0.0
        for o, l in parts:
            w = jnp.exp2(l - top)
            acc = acc + o * w
            total = total + w
        results.append((acc / total).reshape(rows, group, d))
    out_ref[...] = jnp.concatenate(results, axis=1).astype(BF16)


def shards(queries, prefix_keys, prefix_values, suffix_keys, suffix_values, lengths):
    rows, heads, d = queries.shape
    kv_heads = prefix_keys.shape[1]
    group = heads // kv_heads
    span = suffix_keys.shape[1]
    c = d ** (-0.5) * LOG2E
    n = lax.axis_size("ctx")
    cores = 2 if n % 2 == 0 else 1
    chips = n // cores
    m = rows * group
    pieces = -(-3 * kv_heads * (m // d) // 16) * 16

    def shift(x, by):
        return lax.ppermute(x, "ctx", [(i, (i + by) % n) for i in range(n)])

    def call(kernel, out_shape, operands, specs, scratch=(), outs=None, mib=40, name=None, flops=0, moved=0):
        single = not isinstance(out_shape, tuple)
        return pl.pallas_call(
            kernel,
            out_shape=out_shape,
            in_specs=specs,
            out_specs=outs or (VMEM if single else (VMEM,) * len(out_shape)),
            scratch_shapes=scratch,
            compiler_params=pltpu.CompilerParams(vmem_limit_bytes=mib << 20),
            cost_estimate=pl.CostEstimate(flops=flops, bytes_accessed=moved, transcendentals=0),
            name=name,
        )(*operands)

    raw = [prefix_keys.reshape(-1, d), prefix_values.reshape(-1, d)]
    slots = span * kv_heads
    chunk = 128 if span % 128 == 0 else span
    batch = 16
    items = rows * (span // chunk)
    smem = pl.BlockSpec(memory_space=pltpu.SMEM)
    split_queries, table = call(
        partial(queries_kernel, kv_heads=kv_heads, chunk=chunk, chunks=span // chunk, pad=2 * batch),
        (jax.ShapeDtypeStruct((kv_heads, m, d), BF16), jax.ShapeDtypeStruct((items + 2 * batch + 1,), jnp.int32)),
        [pltpu.with_memory_space_constraint(x, pltpu.HBM) for x in (lengths, queries)],
        [pl.BlockSpec(memory_space=pltpu.HBM)] * 2,
        scratch=[pltpu.SMEM((rows,), jnp.int32), pltpu.VMEM((rows, heads, d), BF16), pltpu.SemaphoreType.DMA((2,))],
        outs=(VMEM, smem),
        mib=16,
        name="queries",
        moved=4 * m * kv_heads * d,
    )

    def by_head(x):
        return x.reshape(-1, kv_heads, d).transpose(1, 0, 2)

    visiting = [shift(queries, j * cores) for j in range(1, chips)]

    spread = prefix_keys.shape[0]
    flops = 12 * m * kv_heads * spread * d
    moved = 4 * kv_heads * spread * d

    flat = []
    before = ()
    if cores == 2:
        swap = [(i, i ^ 1) for i in range(n)]
        keys, values = [lax.ppermute(x, "ctx", swap) for x in raw]
        keys = by_head(keys)
        weights = call(
            partial(first_kernel, c=c, kv_heads=kv_heads),
            (jax.ShapeDtypeStruct((kv_heads, m, spread), BF16), jax.ShapeDtypeStruct((kv_heads, m, d), F32)),
            (split_queries, keys),
            [VMEM] * 2,
            mib=24,
            name="first",
            flops=3 * flops // 2,
            moved=moved,
        )
        raw, values, weights = lax.optimization_barrier((raw, values, weights))
        flat = [keys, by_head(values)]
        before = (*weights, flat[1])
    raw = [by_head(x) for x in raw]
    operands = (split_queries, *raw, *before)
    own_o, own_l = call(
        partial(own_kernel, c=c, kv_heads=kv_heads),
        (jax.ShapeDtypeStruct((kv_heads, m, d), F32),) * 2,
        operands,
        [VMEM] * len(operands),
        mib=24,
        name="own",
        flops=flops,
        moved=moved,
    )
    flat = [*flat, *raw]
    visiting, own_o, own_l = lax.optimization_barrier((visiting, own_o, own_l))
    message = jax.ShapeDtypeStruct((kv_heads * m + pieces, d), BF16)
    returned = []
    for j, q in enumerate(visiting):
        msg = call(
            partial(other_kernel, c=c, kv_heads=kv_heads, pieces=pieces),
            message,
            (q, *flat),
            [VMEM] * (1 + len(flat)),
            mib=24,
            name="visiting",
            flops=cores * flops,
            moved=cores * moved,
        )
        returned.append(shift(msg, -(j + 1) * cores))
    local = call(
        partial(suffix_kernel, c=c, kv_heads=kv_heads, batch=batch, chunk=chunk),
        (jax.ShapeDtypeStruct((rows, heads, d), F32),) * 2,
        (lengths, table, queries, suffix_keys.reshape(rows, slots, d), suffix_values.reshape(rows, slots, d), own_o, own_l),
        [smem] * 2 + [VMEM] * 5,
        scratch=[
            pltpu.VMEM((items, heads, d), F32),
            pltpu.VMEM((items, heads, d), F32),
        ],
        mib=12,
        name="suffix",
        flops=4 * rows * heads * slots * d,
        moved=4 * rows * slots * d,
    )
    operands = (*local, *returned)
    return call(
        partial(merge_kernel, kv_heads=kv_heads, group=group),
        jax.ShapeDtypeStruct((rows, heads, d), BF16),
        operands,
        [VMEM] * len(operands),
        mib=16,
        name="merge",
    )


def solution(mesh):
    placed = (
        P(("groups", "ctx"), "head", None),
        P(("groups", "ctx"), "head", None),
        P(("groups", "ctx"), "head", None),
        P(("groups", "ctx"), None, "head", None),
        P(("groups", "ctx"), None, "head", None),
        P(("groups", "ctx")),
    )
    return jax.shard_map(
        shards,
        mesh=mesh,
        in_specs=placed,
        out_specs=P(("groups", "ctx"), "head", None),
        check_vma=False,
    )
```

```python
from functools import partial

import jax
import jax.numpy as jnp
from jax import lax
from jax.experimental import pallas as pl
from jax.experimental.pallas import tpu as pltpu
from jax.sharding import PartitionSpec as P

LOG2E = 1.4426950408889634
F32 = jnp.float32
BF16 = jnp.bfloat16
VMEM = pl.BlockSpec(memory_space=pltpu.VMEM)


def split_heads(q_ref, kv_heads):
    rows, heads, d = q_ref.shape
    group = heads // kv_heads
    wide = q_ref[...].astype(F32)
    return [
        wide[:, h * group : (h + 1) * group, :].reshape(rows * group, d).astype(BF16)
        for h in range(kv_heads)
    ]


def scores_of(q, k):
    return lax.dot_general(q, k, (((1,), (1,)), ((), ())), preferred_element_type=F32)


def attend_blocks(heads_q, kv_refs, c):
    d = heads_q[0].shape[1]
    blocks = len(kv_refs) // 2
    items = [(h, b) for h in range(len(heads_q)) for b in range(blocks)]
    parts = {}
    s = w = None

    def weigh(w, top, v):
        oa = jnp.dot(w, jnp.concatenate([v, jnp.ones_like(v)], axis=1), preferred_element_type=F32)
        return oa[:, :d], oa[:, d:], top

    for step in range(len(items) + 2):
        s_next = w_next = None
        if step < len(items):
            h, b = items[step]
            s_next = scores_of(heads_q[h], kv_refs[2 * b][h])
        if w is not None:
            h, b = items[step - 2]
            parts[h, b] = weigh(*w, kv_refs[2 * b + 1][h])
        if s is not None:
            top = jnp.max(s, axis=1, keepdims=True)
            w_next = (jnp.exp2(s * c - top * c).astype(BF16), top * c)
        s, w = s_next, w_next
    results = []
    for h in range(len(heads_q)):
        mine = [parts[h, b] for b in range(blocks)]
        top = mine[0][2]
        for part in mine[1:]:
            top = jnp.maximum(top, part[2])
        acc = 0.0
        total = 0.0
        for o, l, t in mine:
            scale = jnp.exp2(t - top)
            acc = acc + o * scale
            total = total + l * scale
        results.append((acc / total, top + jnp.log2(total)))
    return results


def lane_eye(n):
    return lax.broadcasted_iota(jnp.int32, (n, n), 0) == lax.broadcasted_iota(jnp.int32, (n, n), 1)


def other_kernel(q_ref, *refs, c, kv_heads, pieces):
    kv_refs, msg_ref = refs[:-1], refs[-1]
    heads_q = split_heads(q_ref, kv_heads)
    m, d = heads_q[0].shape
    eye = lane_eye(d)
    packed = []
    for h, (o, lse) in enumerate(attend_blocks(heads_q, kv_refs, c)):
        msg_ref[h * m : (h + 1) * m, :] = o.astype(BF16)
        packed.append(jnp.sum(jnp.where(eye, lse.reshape(m // d, d, d), 0.0), axis=1))
    rest = jnp.concatenate(packed, axis=0)
    out = []
    for _ in range(3):
        piece = rest.astype(BF16).astype(F32)
        out.append(piece)
        rest = rest - piece
    used = 3 * out[0].shape[0]
    if pieces > used:
        out.append(jnp.zeros((pieces - used, d), F32))
    msg_ref[kv_heads * m :, :] = jnp.concatenate(out, axis=0).astype(BF16)


def first_kernel(q_ref, k_ref, w_ref, top_ref, *, c, kv_heads):
    scores = [scores_of(q_ref[h], k_ref[h]) for h in range(kv_heads)]
    for h in range(kv_heads):
        top = jnp.max(scores[h], axis=1, keepdims=True)
        w_ref[h] = jnp.exp2(scores[h] * c - top * c).astype(BF16)
        top_ref[h] = jnp.broadcast_to(top * c, top_ref.shape[1:])


def late_kernel(w_ref, top_ref, v_ref, o_ref, lse_ref, *, kv_heads):
    d = v_ref.shape[2]
    for h in range(kv_heads):
        v = v_ref[h]
        oa = jnp.dot(w_ref[h], jnp.concatenate([v, jnp.ones_like(v)], axis=1), preferred_element_type=F32)
        o_ref[h] = oa[:, :d] / oa[:, d:]
        lse_ref[h] = top_ref[h] + jnp.log2(oa[:, d:])


def own_kernel(q_ref, k_ref, v_ref, *refs, c, kv_heads):
    before, (o_ref, lse_ref) = refs[:-2], refs[-2:]
    heads_q = [q_ref[h] for h in range(kv_heads)]
    for h, (o, lse) in enumerate(attend_blocks(heads_q, (k_ref, v_ref), c)):
        if before:
            o_old, lse_old = before[0][h], before[1][h]
            top = jnp.maximum(lse, lse_old)
            new, old = jnp.exp2(lse - top), jnp.exp2(lse_old - top)
            total = new + old
            o = (o * new + o_old * old) / total
            lse = top + jnp.log2(total)
        o_ref[h] = o
        lse_ref[h] = jnp.broadcast_to(lse, o.shape)


def queries_kernel(len_hbm, q_hbm, o_ref, item_ref, len_ref, q_ref, sems, *, kv_heads, chunk, chunks, pad):
    numbers = pltpu.make_async_copy(len_hbm, len_ref, sems.at[0])
    numbers.start()
    copy = pltpu.make_async_copy(q_hbm, q_ref, sems.at[1])
    copy.start()
    numbers.wait()
    rows = q_ref.shape[0]

    def enlist(r, count):
        for j in range(chunks):
            item_ref[count + j] = r * chunks + j
        return count + (len_ref[r] + chunk - 1) // chunk

    count = lax.fori_loop(0, rows, enlist, 0, unroll=16 if rows % 16 == 0 else 1)
    for j in range(pad):
        item_ref[count + j] = 0
    item_ref[rows * chunks + pad] = count
    copy.wait()
    for h, q in enumerate(split_heads(q_ref, kv_heads)):
        o_ref[h] = q


def suffix_kernel(
    len_ref, item_ref, q_ref, k_ref, v_ref, op_ref, lp_ref, o_ref, lse_ref, oi_ref, li_ref, *, c, kv_heads, batch, chunk
):
    rows, heads, d = q_ref.shape
    group = heads // kv_heads
    width = chunk * kv_heads
    chunks = k_ref.shape[1] // width
    lane = lax.broadcasted_iota(jnp.int32, (heads, width), 1)
    head = lax.broadcasted_iota(jnp.int32, (heads, width), 0) // group
    place = jnp.where(lane % kv_heads == head, lane // kv_heads, chunk * chunks)

    count = item_ref[rows * chunks + 2 * batch]
    batches = (count + batch - 1) // batch

    def part(slot):
        r = slot // chunks
        j = slot - r * chunks
        return r, j, pl.ds(pl.multiple_of(j * width, width), width)

    def score_batch(i):
        found = []
        for t in range(batch):
            r, _, span = part(item_ref[i * batch + t])
            found.append(scores_of(q_ref[r], k_ref[r, span, :]))
        return tuple(found)

    def finish(i, scores):
        weights = []
        for t in range(batch):
            r, j, _ = part(item_ref[i * batch + t])
            s = jnp.where(place < len_ref[r] - j * chunk, scores[t], -jnp.inf)
            top = jnp.max(s, axis=1, keepdims=True)
            w = jnp.exp2(s * c - top * c).astype(BF16)
            weights.append((w, top * c, jnp.sum(w.astype(F32), axis=1, keepdims=True)))
        for t in range(batch):
            slot = item_ref[i * batch + t]
            r, _, span = part(slot)
            w, top, total = weights[t]
            o = jnp.dot(w, v_ref[r, span, :], preferred_element_type=F32)
            oi_ref[slot] = o * (1.0 / total)
            li_ref[slot] = jnp.broadcast_to(top + jnp.log2(total), (heads, d))

    def body(i, scores):
        ahead = score_batch(i + 1)
        finish(i, scores)
        return ahead

    finish(batches - 1, lax.fori_loop(0, batches - 1, body, score_batch(0)))

    def merge(r, _):
        live = (len_ref[r] + chunk - 1) // chunk
        rows_of = pl.ds(pl.multiple_of(r * group, group), group)
        parts = [
            (
                jnp.concatenate([op_ref[h, rows_of, :] for h in range(kv_heads)], axis=0),
                jnp.concatenate([lp_ref[h, rows_of, :] for h in range(kv_heads)], axis=0),
            )
        ]
        for j in range(chunks):
            slot = r * chunks + j
            parts.append((jnp.where(j < live, oi_ref[slot], 0.0), jnp.where(j < live, li_ref[slot], -jnp.inf)))
        top = parts[0][1]
        for p in parts[1:]:
            top = jnp.maximum(top, p[1])
        acc = 0.0
        total = 0.0
        for o, l in parts:
            w = jnp.exp2(l - top)
            acc = acc + o * w
            total = total + w
        o_ref[r] = acc / total
        lse_ref[r] = top + jnp.log2(total)
        return 0

    lax.fori_loop(0, rows, merge, 0, unroll=16 if rows % 16 == 0 else 1)


def merge_kernel(os_ref, ls_ref, *refs, kv_heads, group):
    msg_refs, out_ref = refs[:-1], refs[-1]
    rows, heads, d = os_ref.shape
    m = rows * group
    n = m // d
    eye = lane_eye(d)
    results = []
    for h in range(kv_heads):
        cols = slice(h * group, (h + 1) * group)
        parts = [(os_ref[:, cols, :].reshape(m, d), ls_ref[:, cols, :].reshape(m, d))]
        for msg in msg_refs:
            o = msg[h * m : (h + 1) * m, :].astype(F32)
            tail = msg[kv_heads * m :, :].astype(F32)
            lse = sum(tail[(p * kv_heads + h) * n : (p * kv_heads + h + 1) * n] for p in range(3))
            lse = jnp.where(eye, jnp.broadcast_to(lse[:, None, :], (n, d, d)), 0.0)
            lse = jnp.sum(lse, axis=2, keepdims=True).reshape(m, 1)
            parts.append((o, jnp.broadcast_to(lse, (m, d))))
        top = parts[0][1]
        for part in parts[1:]:
            top = jnp.maximum(top, part[1])
        acc = 0.0
        total = 0.0
        for o, l in parts:
            w = jnp.exp2(l - top)
            acc = acc + o * w
            total = total + w
        results.append((acc / total).reshape(rows, group, d))
    out_ref[...] = jnp.concatenate(results, axis=1).astype(BF16)


def shards(queries, prefix_keys, prefix_values, suffix_keys, suffix_values, lengths):
    rows, heads, d = queries.shape
    kv_heads = prefix_keys.shape[1]
    group = heads // kv_heads
    span = suffix_keys.shape[1]
    c = d ** (-0.5) * LOG2E
    n = lax.axis_size("ctx")
    cores = 2 if n % 2 == 0 else 1
    chips = n // cores
    m = rows * group
    pieces = -(-3 * kv_heads * (m // d) // 16) * 16

    def shift(x, by):
        return lax.ppermute(x, "ctx", [(i, (i + by) % n) for i in range(n)])

    def call(kernel, out_shape, operands, specs, scratch=(), outs=None, mib=40, name=None, flops=0, moved=0):
        single = not isinstance(out_shape, tuple)
        return pl.pallas_call(
            kernel,
            out_shape=out_shape,
            in_specs=specs,
            out_specs=outs or (VMEM if single else (VMEM,) * len(out_shape)),
            scratch_shapes=scratch,
            compiler_params=pltpu.CompilerParams(vmem_limit_bytes=mib << 20),
            cost_estimate=pl.CostEstimate(flops=flops, bytes_accessed=moved, transcendentals=0),
            name=name,
        )(*operands)

    raw = [prefix_keys.reshape(-1, d), prefix_values.reshape(-1, d)]
    slots = span * kv_heads
    chunk = 128 if span % 128 == 0 else span
    batch = 16
    items = rows * (span // chunk)
    smem = pl.BlockSpec(memory_space=pltpu.SMEM)
    split_queries, table = call(
        partial(queries_kernel, kv_heads=kv_heads, chunk=chunk, chunks=span // chunk, pad=2 * batch),
        (jax.ShapeDtypeStruct((kv_heads, m, d), BF16), jax.ShapeDtypeStruct((items + 2 * batch + 1,), jnp.int32)),
        [pltpu.with_memory_space_constraint(x, pltpu.HBM) for x in (lengths, queries)],
        [pl.BlockSpec(memory_space=pltpu.HBM)] * 2,
        scratch=[pltpu.SMEM((rows,), jnp.int32), pltpu.VMEM((rows, heads, d), BF16), pltpu.SemaphoreType.DMA((2,))],
        outs=(VMEM, smem),
        mib=16,
        name="queries",
        moved=4 * m * kv_heads * d,
    )

    def by_head(x):
        return x.reshape(-1, kv_heads, d).transpose(1, 0, 2)

    visiting = [shift(queries, j * cores) for j in range(1, chips)]

    spread = prefix_keys.shape[0]
    flops = 12 * m * kv_heads * spread * d
    moved = 4 * kv_heads * spread * d

    flat = []
    before = ()
    if cores == 2:
        swap = [(i, i ^ 1) for i in range(n)]
        keys, values = [lax.ppermute(x, "ctx", swap) for x in raw]
        keys = by_head(keys)
        weights = call(
            partial(first_kernel, c=c, kv_heads=kv_heads),
            (jax.ShapeDtypeStruct((kv_heads, m, spread), BF16), jax.ShapeDtypeStruct((kv_heads, m, d), F32)),
            (split_queries, keys),
            [VMEM] * 2,
            mib=24,
            name="first",
            flops=3 * flops // 2,
            moved=moved,
        )
        raw, values, weights = lax.optimization_barrier((raw, values, weights))
        flat = [keys, by_head(values)]
        before = call(
            partial(late_kernel, kv_heads=kv_heads),
            (jax.ShapeDtypeStruct((kv_heads, m, d), F32),) * 2,
            (*weights, flat[1]),
            [VMEM] * 3,
            mib=24,
            name="late",
            flops=flops // 4,
            moved=moved // 2,
        )
    raw = [by_head(x) for x in raw]
    flat = [*flat, *raw]
    visiting, before = lax.optimization_barrier((visiting, before))
    message = jax.ShapeDtypeStruct((kv_heads * m + pieces, d), BF16)
    returned = []
    for j, q in enumerate(visiting):
        msg = call(
            partial(other_kernel, c=c, kv_heads=kv_heads, pieces=pieces),
            message,
            (q, *flat),
            [VMEM] * (1 + len(flat)),
            mib=24,
            name="visiting",
            flops=cores * flops,
            moved=cores * moved,
        )
        returned.append(shift(msg, -(j + 1) * cores))
        raw, msg = lax.optimization_barrier((raw, msg))
    operands = (split_queries, *raw, *before)
    own_o, own_l = call(
        partial(own_kernel, c=c, kv_heads=kv_heads),
        (jax.ShapeDtypeStruct((kv_heads, m, d), F32),) * 2,
        operands,
        [VMEM] * len(operands),
        mib=24,
        name="own",
        flops=flops,
        moved=moved,
    )
    local = call(
        partial(suffix_kernel, c=c, kv_heads=kv_heads, batch=batch, chunk=chunk),
        (jax.ShapeDtypeStruct((rows, heads, d), F32),) * 2,
        (lengths, table, queries, suffix_keys.reshape(rows, slots, d), suffix_values.reshape(rows, slots, d), own_o, own_l),
        [smem] * 2 + [VMEM] * 5,
        scratch=[
            pltpu.VMEM((items, heads, d), F32),
            pltpu.VMEM((items, heads, d), F32),
        ],
        mib=12,
        name="suffix",
        flops=4 * rows * heads * slots * d,
        moved=4 * rows * slots * d,
    )
    operands = (*local, *returned)
    return call(
        partial(merge_kernel, kv_heads=kv_heads, group=group),
        jax.ShapeDtypeStruct((rows, heads, d), BF16),
        operands,
        [VMEM] * len(operands),
        mib=16,
        name="merge",
    )


def solution(mesh):
    placed = (
        P(("groups", "ctx"), "head", None),
        P(("groups", "ctx"), "head", None),
        P(("groups", "ctx"), "head", None),
        P(("groups", "ctx"), None, "head", None),
        P(("groups", "ctx"), None, "head", None),
        P(("groups", "ctx")),
    )
    return jax.shard_map(
        shards,
        mesh=mesh,
        in_specs=placed,
        out_specs=P(("groups", "ctx"), "head", None),
        check_vma=False,
    )
```

```python
from functools import partial

import jax
import jax.numpy as jnp
from jax import lax
from jax.experimental import pallas as pl
from jax.experimental.pallas import tpu as pltpu
from jax.sharding import PartitionSpec as P

LOG2E = 1.4426950408889634
F32 = jnp.float32
BF16 = jnp.bfloat16
VMEM = pl.BlockSpec(memory_space=pltpu.VMEM)


def split_heads(q_ref, kv_heads):
    rows, heads, d = q_ref.shape
    group = heads // kv_heads
    wide = q_ref[...].astype(F32)
    return [
        wide[:, h * group : (h + 1) * group, :].reshape(rows * group, d).astype(BF16)
        for h in range(kv_heads)
    ]


def scores_of(q, k):
    return lax.dot_general(q, k, (((1,), (1,)), ((), ())), preferred_element_type=F32)


def attend_blocks(heads_q, kv_refs, c, ready=()):
    d = heads_q[0].shape[1]
    blocks = len(kv_refs) // 2
    items = [(h, b) for h in range(len(heads_q)) for b in range(blocks)]
    parts = {}
    ready = list(ready)
    s = w = None

    def weigh(w, top, v):
        oa = jnp.dot(w, jnp.concatenate([v, jnp.ones_like(v)], axis=1), preferred_element_type=F32)
        return oa[:, :d], oa[:, d:], top

    def take_ready():
        h, *rest = ready.pop(0)
        parts[h, blocks] = weigh(*rest)

    for step in range(len(items) + 2):
        s_next = w_next = None
        if step < len(items):
            h, b = items[step]
            s_next = scores_of(heads_q[h], kv_refs[2 * b][h])
        if w is not None:
            h, b = items[step - 2]
            parts[h, b] = weigh(*w, kv_refs[2 * b + 1][h])
        elif ready:
            take_ready()
        if s is not None:
            top = jnp.max(s, axis=1, keepdims=True)
            w_next = (jnp.exp2(s * c - top * c).astype(BF16), top * c)
        s, w = s_next, w_next
    while ready:
        take_ready()
    results = []
    for h in range(len(heads_q)):
        mine = [parts[h, b] for b in range(blocks + 1) if (h, b) in parts]
        top = mine[0][2]
        for part in mine[1:]:
            top = jnp.maximum(top, part[2])
        acc = 0.0
        total = 0.0
        for o, l, t in mine:
            scale = jnp.exp2(t - top)
            acc = acc + o * scale
            total = total + l * scale
        results.append((acc / total, top + jnp.log2(total)))
    return results


def lane_eye(n):
    return lax.broadcasted_iota(jnp.int32, (n, n), 0) == lax.broadcasted_iota(jnp.int32, (n, n), 1)


def other_kernel(q_ref, *refs, c, kv_heads, pieces):
    kv_refs, msg_ref = refs[:-1], refs[-1]
    heads_q = split_heads(q_ref, kv_heads)
    m, d = heads_q[0].shape
    eye = lane_eye(d)
    packed = []
    for h, (o, lse) in enumerate(attend_blocks(heads_q, kv_refs, c)):
        msg_ref[h * m : (h + 1) * m, :] = o.astype(BF16)
        packed.append(jnp.sum(jnp.where(eye, lse.reshape(m // d, d, d), 0.0), axis=1))
    rest = jnp.concatenate(packed, axis=0)
    out = []
    for _ in range(3):
        piece = rest.astype(BF16).astype(F32)
        out.append(piece)
        rest = rest - piece
    used = 3 * out[0].shape[0]
    if pieces > used:
        out.append(jnp.zeros((pieces - used, d), F32))
    msg_ref[kv_heads * m :, :] = jnp.concatenate(out, axis=0).astype(BF16)


def first_kernel(q_ref, k_ref, w_ref, top_ref, *, c, kv_heads):
    scores = [scores_of(q_ref[h], k_ref[h]) for h in range(kv_heads)]
    for h in range(kv_heads):
        top = jnp.max(scores[h], axis=1, keepdims=True)
        w_ref[h] = jnp.exp2(scores[h] * c - top * c).astype(BF16)
        top_ref[h] = jnp.broadcast_to(top * c, top_ref.shape[1:])


def own_kernel(q_ref, k_ref, v_ref, *refs, c, kv_heads):
    before, (o_ref, lse_ref) = refs[:-2], refs[-2:]
    heads_q = [q_ref[h] for h in range(kv_heads)]
    ready = ()
    if before:
        w_ref, top_ref, late_ref = before
        ready = [(h, w_ref[h], top_ref[h][:, :1], late_ref[h]) for h in range(kv_heads)]
    for h, (o, lse) in enumerate(attend_blocks(heads_q, (k_ref, v_ref), c, ready)):
        o_ref[h] = o
        lse_ref[h] = jnp.broadcast_to(lse, o.shape)


def queries_kernel(len_hbm, q_hbm, o_ref, item_ref, len_ref, q_ref, sems, *, kv_heads, chunk, chunks, pad):
    numbers = pltpu.make_async_copy(len_hbm, len_ref, sems.at[0])
    numbers.start()
    copy = pltpu.make_async_copy(q_hbm, q_ref, sems.at[1])
    copy.start()
    numbers.wait()
    rows = q_ref.shape[0]

    def enlist(r, count):
        for j in range(chunks):
            item_ref[count + j] = r * chunks + j
        return count + (len_ref[r] + chunk - 1) // chunk

    count = lax.fori_loop(0, rows, enlist, 0, unroll=16 if rows % 16 == 0 else 1)
    for j in range(pad):
        item_ref[count + j] = 0
    item_ref[rows * chunks + pad] = count
    copy.wait()
    for h, q in enumerate(split_heads(q_ref, kv_heads)):
        o_ref[h] = q


def suffix_kernel(
    len_ref, item_ref, q_ref, k_ref, v_ref, op_ref, lp_ref, o_ref, lse_ref, oi_ref, li_ref, *, c, kv_heads, batch, chunk
):
    rows, heads, d = q_ref.shape
    group = heads // kv_heads
    width = chunk * kv_heads
    chunks = k_ref.shape[1] // width
    lane = lax.broadcasted_iota(jnp.int32, (heads, width), 1)
    head = lax.broadcasted_iota(jnp.int32, (heads, width), 0) // group
    place = jnp.where(lane % kv_heads == head, lane // kv_heads, chunk * chunks)

    count = item_ref[rows * chunks + 2 * batch]
    batches = (count + batch - 1) // batch

    def part(slot):
        r = slot // chunks
        j = slot - r * chunks
        return r, j, pl.ds(pl.multiple_of(j * width, width), width)

    def score_batch(i):
        found = []
        for t in range(batch):
            r, _, span = part(item_ref[i * batch + t])
            found.append(scores_of(q_ref[r], k_ref[r, span, :]))
        return tuple(found)

    def finish(i, scores):
        weights = []
        for t in range(batch):
            r, j, _ = part(item_ref[i * batch + t])
            s = jnp.where(place < len_ref[r] - j * chunk, scores[t], -jnp.inf)
            top = jnp.max(s, axis=1, keepdims=True)
            w = jnp.exp2(s * c - top * c).astype(BF16)
            weights.append((w, top * c, jnp.sum(w.astype(F32), axis=1, keepdims=True)))
        for t in range(batch):
            slot = item_ref[i * batch + t]
            r, _, span = part(slot)
            w, top, total = weights[t]
            o = jnp.dot(w, v_ref[r, span, :], preferred_element_type=F32)
            oi_ref[slot] = o * (1.0 / total)
            li_ref[slot] = jnp.broadcast_to(top + jnp.log2(total), (heads, d))

    def body(i, scores):
        ahead = score_batch(i + 1)
        finish(i, scores)
        return ahead

    finish(batches - 1, lax.fori_loop(0, batches - 1, body, score_batch(0)))

    def merge(r, _):
        live = (len_ref[r] + chunk - 1) // chunk
        rows_of = pl.ds(pl.multiple_of(r * group, group), group)
        parts = [
            (
                jnp.concatenate([op_ref[h, rows_of, :] for h in range(kv_heads)], axis=0),
                jnp.concatenate([lp_ref[h, rows_of, :] for h in range(kv_heads)], axis=0),
            )
        ]
        for j in range(chunks):
            slot = r * chunks + j
            parts.append((jnp.where(j < live, oi_ref[slot], 0.0), jnp.where(j < live, li_ref[slot], -jnp.inf)))
        top = parts[0][1]
        for p in parts[1:]:
            top = jnp.maximum(top, p[1])
        acc = 0.0
        total = 0.0
        for o, l in parts:
            w = jnp.exp2(l - top)
            acc = acc + o * w
            total = total + w
        o_ref[r] = acc / total
        lse_ref[r] = top + jnp.log2(total)
        return 0

    lax.fori_loop(0, rows, merge, 0, unroll=16 if rows % 16 == 0 else 1)


def merge_kernel(os_ref, ls_ref, *refs, kv_heads, group):
    msg_refs, out_ref = refs[:-1], refs[-1]
    rows, heads, d = os_ref.shape
    m = rows * group
    n = m // d
    eye = lane_eye(d)
    results = []
    for h in range(kv_heads):
        cols = slice(h * group, (h + 1) * group)
        parts = [(os_ref[:, cols, :].reshape(m, d), ls_ref[:, cols, :].reshape(m, d))]
        for msg in msg_refs:
            o = msg[h * m : (h + 1) * m, :].astype(F32)
            tail = msg[kv_heads * m :, :].astype(F32)
            lse = sum(tail[(p * kv_heads + h) * n : (p * kv_heads + h + 1) * n] for p in range(3))
            lse = jnp.where(eye, jnp.broadcast_to(lse[:, None, :], (n, d, d)), 0.0)
            lse = jnp.sum(lse, axis=2, keepdims=True).reshape(m, 1)
            parts.append((o, jnp.broadcast_to(lse, (m, d))))
        if len(parts) == 2:
            (o, l), (o_far, l_far) = parts
            share = 1.0 / (1.0 + jnp.exp2(jnp.minimum(l - l_far, 126.0)))
            results.append((o + (o_far - o) * share).reshape(rows, group, d))
            continue
        top = parts[0][1]
        for part in parts[1:]:
            top = jnp.maximum(top, part[1])
        acc = 0.0
        total = 0.0
        for o, l in parts:
            w = jnp.exp2(l - top)
            acc = acc + o * w
            total = total + w
        results.append((acc / total).reshape(rows, group, d))
    out_ref[...] = jnp.concatenate(results, axis=1).astype(BF16)


def shards(queries, prefix_keys, prefix_values, suffix_keys, suffix_values, lengths):
    rows, heads, d = queries.shape
    kv_heads = prefix_keys.shape[1]
    group = heads // kv_heads
    span = suffix_keys.shape[1]
    c = d ** (-0.5) * LOG2E
    n = lax.axis_size("ctx")
    cores = 2 if n % 2 == 0 else 1
    chips = n // cores
    m = rows * group
    pieces = -(-3 * kv_heads * (m // d) // 16) * 16

    def shift(x, by):
        return lax.ppermute(x, "ctx", [(i, (i + by) % n) for i in range(n)])

    def call(kernel, out_shape, operands, specs, scratch=(), outs=None, mib=40, name=None, flops=0, moved=0):
        single = not isinstance(out_shape, tuple)
        return pl.pallas_call(
            kernel,
            out_shape=out_shape,
            in_specs=specs,
            out_specs=outs or (VMEM if single else (VMEM,) * len(out_shape)),
            scratch_shapes=scratch,
            compiler_params=pltpu.CompilerParams(vmem_limit_bytes=mib << 20),
            cost_estimate=pl.CostEstimate(flops=flops, bytes_accessed=moved, transcendentals=0),
            name=name,
        )(*operands)

    raw = [prefix_keys.reshape(-1, d), prefix_values.reshape(-1, d)]
    slots = span * kv_heads
    chunk = 128 if span % 128 == 0 else span
    batch = 16
    items = rows * (span // chunk)
    smem = pl.BlockSpec(memory_space=pltpu.SMEM)
    split_queries, table = call(
        partial(queries_kernel, kv_heads=kv_heads, chunk=chunk, chunks=span // chunk, pad=2 * batch),
        (jax.ShapeDtypeStruct((kv_heads, m, d), BF16), jax.ShapeDtypeStruct((items + 2 * batch + 1,), jnp.int32)),
        [pltpu.with_memory_space_constraint(x, pltpu.HBM) for x in (lengths, queries)],
        [pl.BlockSpec(memory_space=pltpu.HBM)] * 2,
        scratch=[pltpu.SMEM((rows,), jnp.int32), pltpu.VMEM((rows, heads, d), BF16), pltpu.SemaphoreType.DMA((2,))],
        outs=(VMEM, smem),
        mib=16,
        name="queries",
        moved=4 * m * kv_heads * d,
    )

    def by_head(x):
        return x.reshape(-1, kv_heads, d).transpose(1, 0, 2)

    visiting = [shift(queries, j * cores) for j in range(1, chips)]

    spread = prefix_keys.shape[0]
    flops = 12 * m * kv_heads * spread * d
    moved = 4 * kv_heads * spread * d

    flat = []
    before = ()
    if cores == 2:
        swap = [(i, i ^ 1) for i in range(n)]
        keys, values = [lax.ppermute(x, "ctx", swap) for x in raw]
        keys = by_head(keys)
        weights = call(
            partial(first_kernel, c=c, kv_heads=kv_heads),
            (jax.ShapeDtypeStruct((kv_heads, m, spread), BF16), jax.ShapeDtypeStruct((kv_heads, m, d), F32)),
            (split_queries, keys),
            [VMEM] * 2,
            mib=24,
            name="first",
            flops=3 * flops // 2,
            moved=moved,
        )
        raw, values, weights = lax.optimization_barrier((raw, values, weights))
        flat = [keys, by_head(values)]
        before = (*weights, flat[1])
    raw = [by_head(x) for x in raw]
    operands = (split_queries, *raw, *before)
    own_o, own_l = call(
        partial(own_kernel, c=c, kv_heads=kv_heads),
        (jax.ShapeDtypeStruct((kv_heads, m, d), F32),) * 2,
        operands,
        [VMEM] * len(operands),
        mib=24,
        name="own",
        flops=flops,
        moved=moved,
    )
    flat = [*flat, *raw]
    visiting, own_o, own_l = lax.optimization_barrier((visiting, own_o, own_l))
    message = jax.ShapeDtypeStruct((kv_heads * m + pieces, d), BF16)
    returned = []
    for j, q in enumerate(visiting):
        msg = call(
            partial(other_kernel, c=c, kv_heads=kv_heads, pieces=pieces),
            message,
            (q, *flat),
            [VMEM] * (1 + len(flat)),
            mib=24,
            name="visiting",
            flops=cores * flops,
            moved=cores * moved,
        )
        returned.append(shift(msg, -(j + 1) * cores))
    local = call(
        partial(suffix_kernel, c=c, kv_heads=kv_heads, batch=batch, chunk=chunk),
        (jax.ShapeDtypeStruct((rows, heads, d), F32),) * 2,
        (lengths, table, queries, suffix_keys.reshape(rows, slots, d), suffix_values.reshape(rows, slots, d), own_o, own_l),
        [smem] * 2 + [VMEM] * 5,
        scratch=[
            pltpu.VMEM((items, heads, d), F32),
            pltpu.VMEM((items, heads, d), F32),
        ],
        mib=12,
        name="suffix",
        flops=4 * rows * heads * slots * d,
        moved=4 * rows * slots * d,
    )
    operands = (*local, *returned)
    return call(
        partial(merge_kernel, kv_heads=kv_heads, group=group),
        jax.ShapeDtypeStruct((rows, heads, d), BF16),
        operands,
        [VMEM] * len(operands),
        mib=16,
        name="merge",
    )


def solution(mesh):
    placed = (
        P(("groups", "ctx"), "head", None),
        P(("groups", "ctx"), "head", None),
        P(("groups", "ctx"), "head", None),
        P(("groups", "ctx"), None, "head", None),
        P(("groups", "ctx"), None, "head", None),
        P(("groups", "ctx")),
    )
    return jax.shard_map(
        shards,
        mesh=mesh,
        in_specs=placed,
        out_specs=P(("groups", "ctx"), "head", None),
        check_vma=False,
    )
```

```python
from functools import partial

import jax
import jax.numpy as jnp
from jax import lax
from jax.experimental import pallas as pl
from jax.experimental.pallas import tpu as pltpu
from jax.sharding import PartitionSpec as P

LOG2E = 1.4426950408889634
F32 = jnp.float32
BF16 = jnp.bfloat16
VMEM = pl.BlockSpec(memory_space=pltpu.VMEM)


def split_heads(q_ref, kv_heads):
    rows, heads, d = q_ref.shape
    group = heads // kv_heads
    wide = q_ref[...].astype(F32)
    return [
        wide[:, h * group : (h + 1) * group, :].reshape(rows * group, d).astype(BF16)
        for h in range(kv_heads)
    ]


def scores_of(q, k):
    return lax.dot_general(q, k, (((1,), (1,)), ((), ())), preferred_element_type=F32)


def attend_blocks(heads_q, kv_refs, c):
    d = heads_q[0].shape[1]
    blocks = len(kv_refs) // 2
    items = [(h, b) for h in range(len(heads_q)) for b in range(blocks)]
    parts = {}
    s = w = None

    def weigh(w, top, v):
        oa = jnp.dot(w, jnp.concatenate([v, jnp.ones_like(v)], axis=1), preferred_element_type=F32)
        return oa[:, :d], oa[:, d:], top

    for step in range(len(items) + 2):
        s_next = w_next = None
        if step < len(items):
            h, b = items[step]
            s_next = scores_of(heads_q[h], kv_refs[2 * b][h])
        if w is not None:
            h, b = items[step - 2]
            parts[h, b] = weigh(*w, kv_refs[2 * b + 1][h])
        if s is not None:
            top = jnp.max(s, axis=1, keepdims=True)
            w_next = (jnp.exp2(s * c - top * c).astype(BF16), top * c)
        s, w = s_next, w_next
    results = []
    for h in range(len(heads_q)):
        mine = [parts[h, b] for b in range(blocks)]
        top = mine[0][2]
        for part in mine[1:]:
            top = jnp.maximum(top, part[2])
        acc = 0.0
        total = 0.0
        for o, l, t in mine:
            scale = jnp.exp2(t - top)
            acc = acc + o * scale
            total = total + l * scale
        results.append((acc / total, top + jnp.log2(total)))
    return results


def lane_eye(n):
    return lax.broadcasted_iota(jnp.int32, (n, n), 0) == lax.broadcasted_iota(jnp.int32, (n, n), 1)


def other_kernel(q_ref, *refs, c, kv_heads, pieces):
    kv_refs, msg_ref = refs[:-1], refs[-1]
    heads_q = split_heads(q_ref, kv_heads)
    m, d = heads_q[0].shape
    eye = lane_eye(d)
    packed = []
    for h, (o, lse) in enumerate(attend_blocks(heads_q, kv_refs, c)):
        msg_ref[h * m : (h + 1) * m, :] = o.astype(BF16)
        packed.append(jnp.sum(jnp.where(eye, lse.reshape(m // d, d, d), 0.0), axis=1))
    rest = jnp.concatenate(packed, axis=0)
    out = []
    for _ in range(3):
        piece = rest.astype(BF16).astype(F32)
        out.append(piece)
        rest = rest - piece
    used = 3 * out[0].shape[0]
    if pieces > used:
        out.append(jnp.zeros((pieces - used, d), F32))
    msg_ref[kv_heads * m :, :] = jnp.concatenate(out, axis=0).astype(BF16)


def weigh_block(q_ref, k_ref, w_ref, top_ref, c):
    kv_heads, m, d = q_ref.shape
    part = m // 2 if m % 32 == 0 else m
    items = [(h, slice(i, i + part)) for h in range(kv_heads) for i in range(0, m, part)]
    s = scores_of(q_ref[items[0][0], items[0][1], :], k_ref[items[0][0]])
    for n, (h, span) in enumerate(items):
        s_next = None
        if n + 1 < len(items):
            h_next, span_next = items[n + 1]
            s_next = scores_of(q_ref[h_next, span_next, :], k_ref[h_next])
        top = jnp.max(s, axis=1, keepdims=True)
        w_ref[h, span, :] = jnp.exp2(s * c - top * c).astype(BF16)
        top_ref[h, span, :] = jnp.broadcast_to(top * c, (part, d))
        s = s_next


def weigh_values(w_ref, top_ref, v_ref, h):
    d = v_ref.shape[2]
    v = v_ref[h]
    oa = jnp.dot(w_ref[h], jnp.concatenate([v, jnp.ones_like(v)], axis=1), preferred_element_type=F32)
    return oa[:, :d], oa[:, d:], top_ref[h]


def first_kernel(q_ref, k_ref, w_ref, top_ref, *, c):
    weigh_block(q_ref, k_ref, w_ref, top_ref, c)


def second_kernel(q_ref, k_ref, w_old, top_old, v_ref, o_ref, l_ref, w_ref, top_ref, *, c):
    for h in range(q_ref.shape[0]):
        o_ref[h], l_ref[h], _ = weigh_values(w_old, top_old, v_ref, h)
    weigh_block(q_ref, k_ref, w_ref, top_ref, c)


def own_kernel(w_ref, top_ref, v_ref, *refs):
    before, (o_ref, lse_ref) = refs[:-2], refs[-2:]
    for h in range(w_ref.shape[0]):
        o, l, top = weigh_values(w_ref, top_ref, v_ref, h)
        if before:
            o_old, l_old, top_old = [x[h] for x in before]
            both = jnp.maximum(top, top_old)
            new, old = jnp.exp2(top - both), jnp.exp2(top_old - both)
            o, l, top = o * new + o_old * old, l * new + l_old * old, both
        o_ref[h] = o / l
        lse_ref[h] = top + jnp.log2(l)


def queries_kernel(len_hbm, q_hbm, o_ref, item_ref, len_ref, q_ref, sems, *, kv_heads, chunk, chunks, pad):
    numbers = pltpu.make_async_copy(len_hbm, len_ref, sems.at[0])
    numbers.start()
    copy = pltpu.make_async_copy(q_hbm, q_ref, sems.at[1])
    copy.start()
    numbers.wait()
    rows = q_ref.shape[0]

    def enlist(r, count):
        for j in range(chunks):
            item_ref[count + j] = r * chunks + j
        return count + (len_ref[r] + chunk - 1) // chunk

    count = lax.fori_loop(0, rows, enlist, 0, unroll=16 if rows % 16 == 0 else 1)
    for j in range(pad):
        item_ref[count + j] = 0
    item_ref[rows * chunks + pad] = count
    copy.wait()
    for h, q in enumerate(split_heads(q_ref, kv_heads)):
        o_ref[h] = q


def suffix_kernel(
    len_ref, item_ref, q_ref, k_ref, v_ref, op_ref, lp_ref, o_ref, lse_ref, oi_ref, li_ref, *, c, kv_heads, batch, chunk
):
    rows, heads, d = q_ref.shape
    group = heads // kv_heads
    width = chunk * kv_heads
    chunks = k_ref.shape[1] // width
    lane = lax.broadcasted_iota(jnp.int32, (heads, width), 1)
    head = lax.broadcasted_iota(jnp.int32, (heads, width), 0) // group
    place = jnp.where(lane % kv_heads == head, lane // kv_heads, chunk * chunks)

    count = item_ref[rows * chunks + 2 * batch]
    batches = (count + batch - 1) // batch

    def part(slot):
        r = slot // chunks
        j = slot - r * chunks
        return r, j, pl.ds(pl.multiple_of(j * width, width), width)

    def score_batch(i):
        found = []
        for t in range(batch):
            r, _, span = part(item_ref[i * batch + t])
            found.append(scores_of(q_ref[r], k_ref[r, span, :]))
        return tuple(found)

    def finish(i, scores):
        weights = []
        for t in range(batch):
            r, j, _ = part(item_ref[i * batch + t])
            s = jnp.where(place < len_ref[r] - j * chunk, scores[t], -jnp.inf)
            top = jnp.max(s, axis=1, keepdims=True)
            w = jnp.exp2(s * c - top * c).astype(BF16)
            weights.append((w, top * c, jnp.sum(w.astype(F32), axis=1, keepdims=True)))
        for t in range(batch):
            slot = item_ref[i * batch + t]
            r, _, span = part(slot)
            w, top, total = weights[t]
            o = jnp.dot(w, v_ref[r, span, :], preferred_element_type=F32)
            oi_ref[slot] = o * (1.0 / total)
            li_ref[slot] = jnp.broadcast_to(top + jnp.log2(total), (heads, d))

    def body(i, scores):
        ahead = score_batch(i + 1)
        finish(i, scores)
        return ahead

    finish(batches - 1, lax.fori_loop(0, batches - 1, body, score_batch(0)))

    def merge(r, _):
        live = (len_ref[r] + chunk - 1) // chunk
        rows_of = pl.ds(pl.multiple_of(r * group, group), group)
        parts = [
            (
                jnp.concatenate([op_ref[h, rows_of, :] for h in range(kv_heads)], axis=0),
                jnp.concatenate([lp_ref[h, rows_of, :] for h in range(kv_heads)], axis=0),
            )
        ]
        for j in range(chunks):
            slot = r * chunks + j
            parts.append((jnp.where(j < live, oi_ref[slot], 0.0), jnp.where(j < live, li_ref[slot], -jnp.inf)))
        top = parts[0][1]
        for p in parts[1:]:
            top = jnp.maximum(top, p[1])
        acc = 0.0
        total = 0.0
        for o, l in parts:
            w = jnp.exp2(l - top)
            acc = acc + o * w
            total = total + w
        o_ref[r] = acc / total
        lse_ref[r] = top + jnp.log2(total)
        return 0

    lax.fori_loop(0, rows, merge, 0, unroll=16 if rows % 16 == 0 else 1)


def merge_kernel(os_ref, ls_ref, *refs, kv_heads, group):
    msg_refs, out_ref = refs[:-1], refs[-1]
    rows, heads, d = os_ref.shape
    m = rows * group
    n = m // d
    eye = lane_eye(d)
    results = []
    for h in range(kv_heads):
        cols = slice(h * group, (h + 1) * group)
        parts = [(os_ref[:, cols, :].reshape(m, d), ls_ref[:, cols, :].reshape(m, d))]
        for msg in msg_refs:
            o = msg[h * m : (h + 1) * m, :].astype(F32)
            tail = msg[kv_heads * m :, :].astype(F32)
            lse = sum(tail[(p * kv_heads + h) * n : (p * kv_heads + h + 1) * n] for p in range(3))
            lse = jnp.where(eye, jnp.broadcast_to(lse[:, None, :], (n, d, d)), 0.0)
            lse = jnp.sum(lse, axis=2, keepdims=True).reshape(m, 1)
            parts.append((o, jnp.broadcast_to(lse, (m, d))))
        if len(parts) == 2:
            (o, l), (o_far, l_far) = parts
            share = 1.0 / (1.0 + jnp.exp2(jnp.minimum(l - l_far, 126.0)))
            results.append((o + (o_far - o) * share).reshape(rows, group, d))
            continue
        top = parts[0][1]
        for part in parts[1:]:
            top = jnp.maximum(top, part[1])
        acc = 0.0
        total = 0.0
        for o, l in parts:
            w = jnp.exp2(l - top)
            acc = acc + o * w
            total = total + w
        results.append((acc / total).reshape(rows, group, d))
    out_ref[...] = jnp.concatenate(results, axis=1).astype(BF16)


def shards(queries, prefix_keys, prefix_values, suffix_keys, suffix_values, lengths):
    rows, heads, d = queries.shape
    kv_heads = prefix_keys.shape[1]
    group = heads // kv_heads
    span = suffix_keys.shape[1]
    c = d ** (-0.5) * LOG2E
    n = lax.axis_size("ctx")
    cores = 2 if n % 2 == 0 else 1
    chips = n // cores
    m = rows * group
    pieces = -(-3 * kv_heads * (m // d) // 16) * 16

    def shift(x, by):
        return lax.ppermute(x, "ctx", [(i, (i + by) % n) for i in range(n)])

    def call(kernel, out_shape, operands, specs, scratch=(), outs=None, mib=40, name=None, flops=0, moved=0):
        single = not isinstance(out_shape, tuple)
        return pl.pallas_call(
            kernel,
            out_shape=out_shape,
            in_specs=specs,
            out_specs=outs or (VMEM if single else (VMEM,) * len(out_shape)),
            scratch_shapes=scratch,
            compiler_params=pltpu.CompilerParams(vmem_limit_bytes=mib << 20),
            cost_estimate=pl.CostEstimate(flops=flops, bytes_accessed=moved, transcendentals=0),
            name=name,
        )(*operands)

    raw = [prefix_keys.reshape(-1, d), prefix_values.reshape(-1, d)]
    slots = span * kv_heads
    chunk = 128 if span % 128 == 0 else span
    batch = 16
    items = rows * (span // chunk)
    smem = pl.BlockSpec(memory_space=pltpu.SMEM)
    split_queries, table = call(
        partial(queries_kernel, kv_heads=kv_heads, chunk=chunk, chunks=span // chunk, pad=2 * batch),
        (jax.ShapeDtypeStruct((kv_heads, m, d), BF16), jax.ShapeDtypeStruct((items + 2 * batch + 1,), jnp.int32)),
        [pltpu.with_memory_space_constraint(x, pltpu.HBM) for x in (lengths, queries)],
        [pl.BlockSpec(memory_space=pltpu.HBM)] * 2,
        scratch=[pltpu.SMEM((rows,), jnp.int32), pltpu.VMEM((rows, heads, d), BF16), pltpu.SemaphoreType.DMA((2,))],
        outs=(VMEM, smem),
        mib=16,
        name="queries",
        moved=4 * m * kv_heads * d,
    )

    def by_head(x):
        return x.reshape(-1, kv_heads, d).transpose(1, 0, 2)

    visiting = [shift(queries, j * cores) for j in range(1, chips)]

    spread = prefix_keys.shape[0]
    flops = 12 * m * kv_heads * spread * d
    moved = 4 * kv_heads * spread * d

    wide = jax.ShapeDtypeStruct((kv_heads, m, d), F32)
    weights_of = (jax.ShapeDtypeStruct((kv_heads, m, spread), BF16), wide)
    flat = []
    before = ()
    if cores == 2:
        swap = [(i, i ^ 1) for i in range(n)]
        keys, values = [lax.ppermute(x, "ctx", swap) for x in raw]
        keys = by_head(keys)
        weights = call(
            partial(first_kernel, c=c),
            weights_of,
            (split_queries, keys),
            [VMEM] * 2,
            mib=20,
            name="first",
            flops=3 * flops // 2,
            moved=moved,
        )
        raw, values, weights = lax.optimization_barrier((raw, values, weights))
        flat = [keys, by_head(values)]
        raw = [by_head(x) for x in raw]
        *before, w, top = call(
            partial(second_kernel, c=c),
            (wide, wide, *weights_of),
            (split_queries, raw[0], *weights, flat[1]),
            [VMEM] * 5,
            mib=20,
            name="second",
            flops=3 * flops // 4,
            moved=moved,
        )
        before = (*before, weights[1])
    else:
        raw = [by_head(x) for x in raw]
        w, top = call(partial(first_kernel, c=c), weights_of, (split_queries, raw[0]), [VMEM] * 2, mib=20, name="first")
    flat = [*flat, *raw]
    visiting, w, before = lax.optimization_barrier((visiting, w, before))
    message = jax.ShapeDtypeStruct((kv_heads * m + pieces, d), BF16)
    returned = []
    for j, q in enumerate(visiting):
        msg = call(
            partial(other_kernel, c=c, kv_heads=kv_heads, pieces=pieces),
            message,
            (q, *flat),
            [VMEM] * (1 + len(flat)),
            mib=24,
            name="visiting",
            flops=cores * flops,
            moved=cores * moved,
        )
        returned.append(shift(msg, -(j + 1) * cores))
        w, msg = lax.optimization_barrier((w, msg))
    operands = (w, top, raw[1], *before)
    own_o, own_l = call(
        own_kernel,
        (wide,) * 2,
        operands,
        [VMEM] * len(operands),
        mib=16,
        name="own",
        flops=flops // 4,
        moved=moved // 2,
    )
    local = call(
        partial(suffix_kernel, c=c, kv_heads=kv_heads, batch=batch, chunk=chunk),
        (jax.ShapeDtypeStruct((rows, heads, d), F32),) * 2,
        (lengths, table, queries, suffix_keys.reshape(rows, slots, d), suffix_values.reshape(rows, slots, d), own_o, own_l),
        [smem] * 2 + [VMEM] * 5,
        scratch=[
            pltpu.VMEM((items, heads, d), F32),
            pltpu.VMEM((items, heads, d), F32),
        ],
        mib=12,
        name="suffix",
        flops=4 * rows * heads * slots * d,
        moved=4 * rows * slots * d,
    )
    operands = (*local, *returned)
    return call(
        partial(merge_kernel, kv_heads=kv_heads, group=group),
        jax.ShapeDtypeStruct((rows, heads, d), BF16),
        operands,
        [VMEM] * len(operands),
        mib=16,
        name="merge",
    )


def solution(mesh):
    placed = (
        P(("groups", "ctx"), "head", None),
        P(("groups", "ctx"), "head", None),
        P(("groups", "ctx"), "head", None),
        P(("groups", "ctx"), None, "head", None),
        P(("groups", "ctx"), None, "head", None),
        P(("groups", "ctx")),
    )
    return jax.shard_map(
        shards,
        mesh=mesh,
        in_specs=placed,
        out_specs=P(("groups", "ctx"), "head", None),
        check_vma=False,
    )
```

```python
from functools import partial

import jax
import jax.numpy as jnp
from jax import lax
from jax.experimental import pallas as pl
from jax.experimental.pallas import tpu as pltpu
from jax.sharding import PartitionSpec as P

LOG2E = 1.4426950408889634
F32 = jnp.float32
BF16 = jnp.bfloat16
VMEM = pl.BlockSpec(memory_space=pltpu.VMEM)


def split_heads(q_ref, kv_heads):
    rows, heads, d = q_ref.shape
    group = heads // kv_heads
    wide = q_ref[...].astype(F32)
    return [
        wide[:, h * group : (h + 1) * group, :].reshape(rows * group, d).astype(BF16)
        for h in range(kv_heads)
    ]


def scores_of(q, k):
    return lax.dot_general(q, k, (((1,), (1,)), ((), ())), preferred_element_type=F32)


def attend_blocks(heads_q, kv_refs, c):
    d = heads_q[0].shape[1]
    blocks = len(kv_refs) // 2
    items = [(h, b) for h in range(len(heads_q)) for b in range(blocks)]
    parts = {}
    s = w = None

    def weigh(w, top, v):
        oa = jnp.dot(w, jnp.concatenate([v, jnp.ones_like(v)], axis=1), preferred_element_type=F32)
        return oa[:, :d], oa[:, d:], top

    for step in range(len(items) + 2):
        s_next = w_next = None
        if step < len(items):
            h, b = items[step]
            s_next = scores_of(heads_q[h], kv_refs[2 * b][h])
        if w is not None:
            h, b = items[step - 2]
            parts[h, b] = weigh(*w, kv_refs[2 * b + 1][h])
        if s is not None:
            top = jnp.max(s, axis=1, keepdims=True)
            w_next = (jnp.exp2(s * c - top * c).astype(BF16), top * c)
        s, w = s_next, w_next
    results = []
    for h in range(len(heads_q)):
        mine = [parts[h, b] for b in range(blocks)]
        top = mine[0][2]
        for part in mine[1:]:
            top = jnp.maximum(top, part[2])
        acc = 0.0
        total = 0.0
        for o, l, t in mine:
            scale = jnp.exp2(t - top)
            acc = acc + o * scale
            total = total + l * scale
        results.append((acc / total, top + jnp.log2(total)))
    return results


def lane_eye(n):
    return lax.broadcasted_iota(jnp.int32, (n, n), 0) == lax.broadcasted_iota(jnp.int32, (n, n), 1)


def other_kernel(q_ref, *refs, c, kv_heads, pieces):
    kv_refs, msg_ref = refs[:-1], refs[-1]
    heads_q = split_heads(q_ref, kv_heads)
    m, d = heads_q[0].shape
    eye = lane_eye(d)
    packed = []
    for h, (o, lse) in enumerate(attend_blocks(heads_q, kv_refs, c)):
        msg_ref[h * m : (h + 1) * m, :] = o.astype(BF16)
        packed.append(jnp.sum(jnp.where(eye, lse.reshape(m // d, d, d), 0.0), axis=1))
    rest = jnp.concatenate(packed, axis=0)
    out = []
    for _ in range(3):
        piece = rest.astype(BF16).astype(F32)
        out.append(piece)
        rest = rest - piece
    used = 3 * out[0].shape[0]
    if pieces > used:
        out.append(jnp.zeros((pieces - used, d), F32))
    msg_ref[kv_heads * m :, :] = jnp.concatenate(out, axis=0).astype(BF16)


def weigh_block(q_ref, k_ref, w_ref, top_ref, c, between=()):
    kv_heads, m, d = q_ref.shape
    part = m // 2 if m % 32 == 0 else m
    items = [(h, slice(i, i + part)) for h in range(kv_heads) for i in range(0, m, part)]
    s = scores_of(q_ref[items[0][0], items[0][1], :], k_ref[items[0][0]])
    between = list(between)
    for n, (h, span) in enumerate(items):
        s_next = None
        if n + 1 < len(items):
            h_next, span_next = items[n + 1]
            s_next = scores_of(q_ref[h_next, span_next, :], k_ref[h_next])
        while len(between) >= len(items) - n:
            between.pop(0)()
        top = jnp.max(s, axis=1, keepdims=True)
        w_ref[h, span, :] = jnp.exp2(s * c - top * c).astype(BF16)
        top_ref[h, span, :] = jnp.broadcast_to(top * c, (part, d))
        s = s_next


def weigh_values(w_ref, top_ref, v_ref, h):
    d = v_ref.shape[2]
    v = v_ref[h]
    oa = jnp.dot(w_ref[h], jnp.concatenate([v, jnp.ones_like(v)], axis=1), preferred_element_type=F32)
    return oa[:, :d], oa[:, d:], top_ref[h]


def first_kernel(q_ref, k_ref, w_ref, top_ref, *, c):
    weigh_block(q_ref, k_ref, w_ref, top_ref, c)


def second_kernel(q_ref, k_ref, w_old, top_old, v_ref, o_ref, l_ref, w_ref, top_ref, *, c):
    def late(h):
        o_ref[h], l_ref[h], _ = weigh_values(w_old, top_old, v_ref, h)

    weigh_block(q_ref, k_ref, w_ref, top_ref, c, [partial(late, h) for h in range(q_ref.shape[0])])


def own_kernel(w_ref, top_ref, v_ref, *refs):
    before, (o_ref, lse_ref) = refs[:-2], refs[-2:]
    for h in range(w_ref.shape[0]):
        o, l, top = weigh_values(w_ref, top_ref, v_ref, h)
        if before:
            o_old, l_old, top_old = [x[h] for x in before]
            both = jnp.maximum(top, top_old)
            new, old = jnp.exp2(top - both), jnp.exp2(top_old - both)
            o, l, top = o * new + o_old * old, l * new + l_old * old, both
        o_ref[h] = o / l
        lse_ref[h] = top + jnp.log2(l)


def queries_kernel(len_hbm, q_hbm, o_ref, item_ref, len_ref, q_ref, sems, *, kv_heads, chunk, chunks, pad):
    numbers = pltpu.make_async_copy(len_hbm, len_ref, sems.at[0])
    numbers.start()
    copy = pltpu.make_async_copy(q_hbm, q_ref, sems.at[1])
    copy.start()
    numbers.wait()
    rows = q_ref.shape[0]

    def enlist(r, count):
        for j in range(chunks):
            item_ref[count + j] = r * chunks + j
        return count + (len_ref[r] + chunk - 1) // chunk

    count = lax.fori_loop(0, rows, enlist, 0, unroll=16 if rows % 16 == 0 else 1)
    for j in range(pad):
        item_ref[count + j] = 0
    item_ref[rows * chunks + pad] = count
    copy.wait()
    for h, q in enumerate(split_heads(q_ref, kv_heads)):
        o_ref[h] = q


def suffix_kernel(
    len_ref, item_ref, q_ref, k_ref, v_ref, op_ref, lp_ref, o_ref, lse_ref, oi_ref, li_ref, *, c, kv_heads, batch, chunk
):
    rows, heads, d = q_ref.shape
    group = heads // kv_heads
    width = chunk * kv_heads
    chunks = k_ref.shape[1] // width
    lane = lax.broadcasted_iota(jnp.int32, (heads, width), 1)
    head = lax.broadcasted_iota(jnp.int32, (heads, width), 0) // group
    place = jnp.where(lane % kv_heads == head, lane // kv_heads, chunk * chunks)

    count = item_ref[rows * chunks + 2 * batch]
    batches = (count + batch - 1) // batch

    def part(slot):
        r = slot // chunks
        j = slot - r * chunks
        return r, j, pl.ds(pl.multiple_of(j * width, width), width)

    def score_batch(i):
        found = []
        for t in range(batch):
            r, _, span = part(item_ref[i * batch + t])
            found.append(scores_of(q_ref[r], k_ref[r, span, :]))
        return tuple(found)

    def finish(i, scores):
        weights = []
        for t in range(batch):
            r, j, _ = part(item_ref[i * batch + t])
            s = jnp.where(place < len_ref[r] - j * chunk, scores[t], -jnp.inf)
            top = jnp.max(s, axis=1, keepdims=True)
            w = jnp.exp2(s * c - top * c).astype(BF16)
            weights.append((w, top * c, jnp.sum(w.astype(F32), axis=1, keepdims=True)))
        for t in range(batch):
            slot = item_ref[i * batch + t]
            r, _, span = part(slot)
            w, top, total = weights[t]
            o = jnp.dot(w, v_ref[r, span, :], preferred_element_type=F32)
            oi_ref[slot] = o * (1.0 / total)
            li_ref[slot] = jnp.broadcast_to(top + jnp.log2(total), (heads, d))

    def body(i, scores):
        ahead = score_batch(i + 1)
        finish(i, scores)
        return ahead

    finish(batches - 1, lax.fori_loop(0, batches - 1, body, score_batch(0)))

    def merge(r, _):
        live = (len_ref[r] + chunk - 1) // chunk
        rows_of = pl.ds(pl.multiple_of(r * group, group), group)
        parts = [
            (
                jnp.concatenate([op_ref[h, rows_of, :] for h in range(kv_heads)], axis=0),
                jnp.concatenate([lp_ref[h, rows_of, :] for h in range(kv_heads)], axis=0),
            )
        ]
        for j in range(chunks):
            slot = r * chunks + j
            parts.append((jnp.where(j < live, oi_ref[slot], 0.0), jnp.where(j < live, li_ref[slot], -jnp.inf)))
        top = parts[0][1]
        for p in parts[1:]:
            top = jnp.maximum(top, p[1])
        acc = 0.0
        total = 0.0
        for o, l in parts:
            w = jnp.exp2(l - top)
            acc = acc + o * w
            total = total + w
        o_ref[r] = acc / total
        lse_ref[r] = top + jnp.log2(total)
        return 0

    lax.fori_loop(0, rows, merge, 0, unroll=16 if rows % 16 == 0 else 1)


def merge_kernel(os_ref, ls_ref, *refs, kv_heads, group):
    msg_refs, out_ref = refs[:-1], refs[-1]
    rows, heads, d = os_ref.shape
    m = rows * group
    n = m // d
    eye = lane_eye(d)
    results = []
    for h in range(kv_heads):
        cols = slice(h * group, (h + 1) * group)
        parts = [(os_ref[:, cols, :].reshape(m, d), ls_ref[:, cols, :].reshape(m, d))]
        for msg in msg_refs:
            o = msg[h * m : (h + 1) * m, :].astype(F32)
            tail = msg[kv_heads * m :, :].astype(F32)
            lse = sum(tail[(p * kv_heads + h) * n : (p * kv_heads + h + 1) * n] for p in range(3))
            lse = jnp.where(eye, jnp.broadcast_to(lse[:, None, :], (n, d, d)), 0.0)
            lse = jnp.sum(lse, axis=2, keepdims=True).reshape(m, 1)
            parts.append((o, jnp.broadcast_to(lse, (m, d))))
        if len(parts) == 2:
            (o, l), (o_far, l_far) = parts
            share = 1.0 / (1.0 + jnp.exp2(jnp.minimum(l - l_far, 126.0)))
            results.append((o + (o_far - o) * share).reshape(rows, group, d))
            continue
        top = parts[0][1]
        for part in parts[1:]:
            top = jnp.maximum(top, part[1])
        acc = 0.0
        total = 0.0
        for o, l in parts:
            w = jnp.exp2(l - top)
            acc = acc + o * w
            total = total + w
        results.append((acc / total).reshape(rows, group, d))
    out_ref[...] = jnp.concatenate(results, axis=1).astype(BF16)


def shards(queries, prefix_keys, prefix_values, suffix_keys, suffix_values, lengths):
    rows, heads, d = queries.shape
    kv_heads = prefix_keys.shape[1]
    group = heads // kv_heads
    span = suffix_keys.shape[1]
    c = d ** (-0.5) * LOG2E
    n = lax.axis_size("ctx")
    cores = 2 if n % 2 == 0 else 1
    chips = n // cores
    m = rows * group
    pieces = -(-3 * kv_heads * (m // d) // 16) * 16

    def shift(x, by):
        return lax.ppermute(x, "ctx", [(i, (i + by) % n) for i in range(n)])

    def call(kernel, out_shape, operands, specs, scratch=(), outs=None, mib=40, name=None, flops=0, moved=0):
        single = not isinstance(out_shape, tuple)
        return pl.pallas_call(
            kernel,
            out_shape=out_shape,
            in_specs=specs,
            out_specs=outs or (VMEM if single else (VMEM,) * len(out_shape)),
            scratch_shapes=scratch,
            compiler_params=pltpu.CompilerParams(vmem_limit_bytes=mib << 20),
            cost_estimate=pl.CostEstimate(flops=flops, bytes_accessed=moved, transcendentals=0),
            name=name,
        )(*operands)

    raw = [prefix_keys.reshape(-1, d), prefix_values.reshape(-1, d)]
    slots = span * kv_heads
    chunk = 128 if span % 128 == 0 else span
    batch = 16
    items = rows * (span // chunk)
    smem = pl.BlockSpec(memory_space=pltpu.SMEM)
    split_queries, table = call(
        partial(queries_kernel, kv_heads=kv_heads, chunk=chunk, chunks=span // chunk, pad=2 * batch),
        (jax.ShapeDtypeStruct((kv_heads, m, d), BF16), jax.ShapeDtypeStruct((items + 2 * batch + 1,), jnp.int32)),
        [pltpu.with_memory_space_constraint(x, pltpu.HBM) for x in (lengths, queries)],
        [pl.BlockSpec(memory_space=pltpu.HBM)] * 2,
        scratch=[pltpu.SMEM((rows,), jnp.int32), pltpu.VMEM((rows, heads, d), BF16), pltpu.SemaphoreType.DMA((2,))],
        outs=(VMEM, smem),
        mib=16,
        name="queries",
        moved=4 * m * kv_heads * d,
    )

    def by_head(x):
        return x.reshape(-1, kv_heads, d).transpose(1, 0, 2)

    visiting = [shift(queries, j * cores) for j in range(1, chips)]

    spread = prefix_keys.shape[0]
    flops = 12 * m * kv_heads * spread * d
    moved = 4 * kv_heads * spread * d

    wide = jax.ShapeDtypeStruct((kv_heads, m, d), F32)
    weights_of = (jax.ShapeDtypeStruct((kv_heads, m, spread), BF16), wide)
    flat = []
    before = ()
    if cores == 2:
        swap = [(i, i ^ 1) for i in range(n)]
        keys, values = [lax.ppermute(x, "ctx", swap) for x in raw]
        keys = by_head(keys)
        weights = call(
            partial(first_kernel, c=c),
            weights_of,
            (split_queries, keys),
            [VMEM] * 2,
            mib=20,
            name="first",
            flops=3 * flops // 2,
            moved=moved,
        )
        raw, values, weights = lax.optimization_barrier((raw, values, weights))
        flat = [keys, by_head(values)]
        raw = [by_head(x) for x in raw]
        *before, w, top = call(
            partial(second_kernel, c=c),
            (wide, wide, *weights_of),
            (split_queries, raw[0], *weights, flat[1]),
            [VMEM] * 5,
            mib=20,
            name="second",
            flops=3 * flops // 4,
            moved=moved,
        )
        before = (*before, weights[1])
    else:
        raw = [by_head(x) for x in raw]
        w, top = call(partial(first_kernel, c=c), weights_of, (split_queries, raw[0]), [VMEM] * 2, mib=20, name="first")
    flat = [*flat, *raw]
    visiting, w, before = lax.optimization_barrier((visiting, w, before))
    message = jax.ShapeDtypeStruct((kv_heads * m + pieces, d), BF16)
    returned = []
    for j, q in enumerate(visiting):
        msg = call(
            partial(other_kernel, c=c, kv_heads=kv_heads, pieces=pieces),
            message,
            (q, *flat),
            [VMEM] * (1 + len(flat)),
            mib=24,
            name="visiting",
            flops=cores * flops,
            moved=cores * moved,
        )
        returned.append(shift(msg, -(j + 1) * cores))
        w, msg = lax.optimization_barrier((w, msg))
    operands = (w, top, raw[1], *before)
    own_o, own_l = call(
        own_kernel,
        (wide,) * 2,
        operands,
        [VMEM] * len(operands),
        mib=16,
        name="own",
        flops=flops // 4,
        moved=moved // 2,
    )
    local = call(
        partial(suffix_kernel, c=c, kv_heads=kv_heads, batch=batch, chunk=chunk),
        (jax.ShapeDtypeStruct((rows, heads, d), F32),) * 2,
        (lengths, table, queries, suffix_keys.reshape(rows, slots, d), suffix_values.reshape(rows, slots, d), own_o, own_l),
        [smem] * 2 + [VMEM] * 5,
        scratch=[
            pltpu.VMEM((items, heads, d), F32),
            pltpu.VMEM((items, heads, d), F32),
        ],
        mib=12,
        name="suffix",
        flops=4 * rows * heads * slots * d,
        moved=4 * rows * slots * d,
    )
    operands = (*local, *returned)
    return call(
        partial(merge_kernel, kv_heads=kv_heads, group=group),
        jax.ShapeDtypeStruct((rows, heads, d), BF16),
        operands,
        [VMEM] * len(operands),
        mib=16,
        name="merge",
    )


def solution(mesh):
    placed = (
        P(("groups", "ctx"), "head", None),
        P(("groups", "ctx"), "head", None),
        P(("groups", "ctx"), "head", None),
        P(("groups", "ctx"), None, "head", None),
        P(("groups", "ctx"), None, "head", None),
        P(("groups", "ctx")),
    )
    return jax.shard_map(
        shards,
        mesh=mesh,
        in_specs=placed,
        out_specs=P(("groups", "ctx"), "head", None),
        check_vma=False,
    )
```

```python
from functools import partial

import jax
import jax.numpy as jnp
from jax import lax
from jax.experimental import pallas as pl
from jax.experimental.pallas import tpu as pltpu
from jax.sharding import PartitionSpec as P

LOG2E = 1.4426950408889634
F32 = jnp.float32
BF16 = jnp.bfloat16
VMEM = pl.BlockSpec(memory_space=pltpu.VMEM)


def split_heads(q_ref, kv_heads):
    rows, heads, d = q_ref.shape
    group = heads // kv_heads
    wide = q_ref[...].astype(F32)
    return [
        wide[:, h * group : (h + 1) * group, :].reshape(rows * group, d).astype(BF16)
        for h in range(kv_heads)
    ]


def scores_of(q, k):
    return lax.dot_general(q, k, (((1,), (1,)), ((), ())), preferred_element_type=F32)


def attend_blocks(heads_q, kv_refs, c, ready=()):
    d = heads_q[0].shape[1]
    blocks = len(kv_refs) // 2
    items = [(h, b) for h in range(len(heads_q)) for b in range(blocks)]
    parts = {}
    ready = list(ready)
    s = w = None

    def weigh(w, top, v):
        oa = jnp.dot(w, jnp.concatenate([v, jnp.ones_like(v)], axis=1), preferred_element_type=F32)
        return oa[:, :d], oa[:, d:], top

    def take_ready():
        h, *rest = ready.pop(0)
        parts[h, blocks] = weigh(*rest)

    for step in range(len(items) + 2):
        s_next = w_next = None
        if step < len(items):
            h, b = items[step]
            s_next = scores_of(heads_q[h], kv_refs[2 * b][h])
        if w is not None:
            h, b = items[step - 2]
            parts[h, b] = weigh(*w, kv_refs[2 * b + 1][h])
        elif ready:
            take_ready()
        if s is not None:
            top = jnp.max(s, axis=1, keepdims=True)
            w_next = (jnp.exp2(s * c - top * c).astype(BF16), top * c)
        s, w = s_next, w_next
    while ready:
        take_ready()
    results = []
    for h in range(len(heads_q)):
        mine = [parts[h, b] for b in range(blocks + 1) if (h, b) in parts]
        top = mine[0][2]
        for part in mine[1:]:
            top = jnp.maximum(top, part[2])
        acc = 0.0
        total = 0.0
        for o, l, t in mine:
            scale = jnp.exp2(t - top)
            acc = acc + o * scale
            total = total + l * scale
        results.append((acc / total, top + jnp.log2(total)))
    return results


def lane_eye(n):
    return lax.broadcasted_iota(jnp.int32, (n, n), 0) == lax.broadcasted_iota(jnp.int32, (n, n), 1)


def other_kernel(q_ref, *refs, c, kv_heads, pieces):
    kv_refs, msg_ref = refs[:-1], refs[-1]
    heads_q = split_heads(q_ref, kv_heads)
    m, d = heads_q[0].shape
    eye = lane_eye(d)
    packed = []
    for h, (o, lse) in enumerate(attend_blocks(heads_q, kv_refs, c)):
        msg_ref[h * m : (h + 1) * m, :] = o.astype(BF16)
        packed.append(jnp.sum(jnp.where(eye, lse.reshape(m // d, d, d), 0.0), axis=1))
    rest = jnp.concatenate(packed, axis=0)
    out = []
    for _ in range(3):
        piece = rest.astype(BF16).astype(F32)
        out.append(piece)
        rest = rest - piece
    used = 3 * out[0].shape[0]
    if pieces > used:
        out.append(jnp.zeros((pieces - used, d), F32))
    msg_ref[kv_heads * m :, :] = jnp.concatenate(out, axis=0).astype(BF16)


def first_kernel(q_ref, k_ref, w_ref, top_ref, *, c, kv_heads):
    scores = [scores_of(q_ref[h], k_ref[h]) for h in range(kv_heads)]
    for h in range(kv_heads):
        top = jnp.max(scores[h], axis=1, keepdims=True)
        w_ref[h] = jnp.exp2(scores[h] * c - top * c).astype(BF16)
        top_ref[h] = jnp.broadcast_to(top * c, top_ref.shape[1:])


def own_kernel(q_ref, k_ref, v_ref, *refs, c, kv_heads):
    before, (o_ref, lse_ref) = refs[:-2], refs[-2:]
    heads_q = [q_ref[h] for h in range(kv_heads)]
    ready = ()
    if before:
        w_ref, top_ref, late_ref = before
        ready = [(h, w_ref[h], top_ref[h][:, :1], late_ref[h]) for h in range(kv_heads)]
    for h, (o, lse) in enumerate(attend_blocks(heads_q, (k_ref, v_ref), c, ready)):
        o_ref[h] = o
        lse_ref[h] = jnp.broadcast_to(lse, o.shape)


def queries_kernel(len_hbm, q_hbm, o_ref, item_ref, len_ref, q_ref, sems, *, kv_heads, chunk, chunks, pad):
    numbers = pltpu.make_async_copy(len_hbm, len_ref, sems.at[0])
    numbers.start()
    copy = pltpu.make_async_copy(q_hbm, q_ref, sems.at[1])
    copy.start()
    numbers.wait()
    rows = q_ref.shape[0]

    def enlist(r, count):
        for j in range(chunks):
            item_ref[count + j] = r * chunks + j
        return count + (len_ref[r] + chunk - 1) // chunk

    count = lax.fori_loop(0, rows, enlist, 0, unroll=16 if rows % 16 == 0 else 1)
    for j in range(pad):
        item_ref[count + j] = 0
    item_ref[rows * chunks + pad] = count
    copy.wait()
    for h, q in enumerate(split_heads(q_ref, kv_heads)):
        o_ref[h] = q


def suffix_kernel(
    len_ref, item_ref, q_ref, k_ref, v_ref, op_ref, lp_ref, o_ref, lse_ref, oi_ref, li_ref, *, c, kv_heads, batch, chunk
):
    rows, heads, d = q_ref.shape
    group = heads // kv_heads
    width = chunk * kv_heads
    chunks = k_ref.shape[1] // width
    lane = lax.broadcasted_iota(jnp.int32, (heads, width), 1)
    head = lax.broadcasted_iota(jnp.int32, (heads, width), 0) // group
    place = jnp.where(lane % kv_heads == head, lane // kv_heads, chunk * chunks)

    count = item_ref[rows * chunks + 2 * batch]
    batches = (count + batch - 1) // batch

    def part(slot):
        r = slot // chunks
        j = slot - r * chunks
        return r, j, pl.ds(pl.multiple_of(j * width, width), width)

    def score_batch(i):
        found = []
        for t in range(batch):
            r, _, span = part(item_ref[i * batch + t])
            found.append(scores_of(q_ref[r], k_ref[r, span, :]))
        return tuple(found)

    def finish(i, scores):
        weights = []
        for t in range(batch):
            r, j, _ = part(item_ref[i * batch + t])
            s = jnp.where(place < len_ref[r] - j * chunk, scores[t], -jnp.inf)
            top = jnp.max(s, axis=1, keepdims=True)
            w = jnp.exp2(s * c - top * c).astype(BF16)
            weights.append((w, top * c, jnp.sum(w.astype(F32), axis=1, keepdims=True)))
        for t in range(batch):
            slot = item_ref[i * batch + t]
            r, _, span = part(slot)
            w, top, total = weights[t]
            o = jnp.dot(w, v_ref[r, span, :], preferred_element_type=F32)
            oi_ref[slot] = o * (1.0 / total)
            li_ref[slot] = jnp.broadcast_to(top + jnp.log2(total), (heads, d))

    def body(i, scores):
        ahead = score_batch(i + 1)
        finish(i, scores)
        return ahead

    finish(batches - 1, lax.fori_loop(0, batches - 1, body, score_batch(0)))

    def merge(r, _):
        live = (len_ref[r] + chunk - 1) // chunk
        rows_of = pl.ds(pl.multiple_of(r * group, group), group)
        parts = [
            (
                jnp.concatenate([op_ref[h, rows_of, :] for h in range(kv_heads)], axis=0),
                jnp.concatenate([lp_ref[h, rows_of, :] for h in range(kv_heads)], axis=0),
            )
        ]
        for j in range(chunks):
            slot = r * chunks + j
            parts.append((jnp.where(j < live, oi_ref[slot], 0.0), jnp.where(j < live, li_ref[slot], -jnp.inf)))
        top = parts[0][1]
        for p in parts[1:]:
            top = jnp.maximum(top, p[1])
        acc = 0.0
        total = 0.0
        for o, l in parts:
            w = jnp.exp2(l - top)
            acc = acc + o * w
            total = total + w
        o_ref[r] = acc / total
        lse_ref[r] = top + jnp.log2(total)
        return 0

    lax.fori_loop(0, rows, merge, 0, unroll=16 if rows % 16 == 0 else 1)


def merge_kernel(os_ref, ls_ref, *refs, kv_heads, group):
    msg_refs, out_ref = refs[:-1], refs[-1]
    rows, heads, d = os_ref.shape
    m = rows * group
    n = m // d
    eye = lane_eye(d)
    results = []
    for h in range(kv_heads):
        cols = slice(h * group, (h + 1) * group)
        parts = [(os_ref[:, cols, :].reshape(m, d), ls_ref[:, cols, :].reshape(m, d))]
        for msg in msg_refs:
            o = msg[h * m : (h + 1) * m, :].astype(F32)
            tail = msg[kv_heads * m :, :].astype(F32)
            lse = sum(tail[(p * kv_heads + h) * n : (p * kv_heads + h + 1) * n] for p in range(3))
            lse = jnp.where(eye, jnp.broadcast_to(lse[:, None, :], (n, d, d)), 0.0)
            lse = jnp.sum(lse, axis=2, keepdims=True).reshape(m, 1)
            parts.append((o, jnp.broadcast_to(lse, (m, d))))
        if len(parts) == 2:
            (o, l), (o_far, l_far) = parts
            share = 1.0 / (1.0 + jnp.exp2(jnp.minimum(l - l_far, 126.0)))
            results.append((o + (o_far - o) * share).reshape(rows, group, d))
            continue
        top = parts[0][1]
        for part in parts[1:]:
            top = jnp.maximum(top, part[1])
        acc = 0.0
        total = 0.0
        for o, l in parts:
            w = jnp.exp2(l - top)
            acc = acc + o * w
            total = total + w
        results.append((acc / total).reshape(rows, group, d))
    out_ref[...] = jnp.concatenate(results, axis=1).astype(BF16)


def shards(queries, prefix_keys, prefix_values, suffix_keys, suffix_values, lengths):
    rows, heads, d = queries.shape
    kv_heads = prefix_keys.shape[1]
    group = heads // kv_heads
    span = suffix_keys.shape[1]
    c = d ** (-0.5) * LOG2E
    n = lax.axis_size("ctx")
    cores = 2 if n % 2 == 0 else 1
    chips = n // cores
    m = rows * group
    pieces = -(-3 * kv_heads * (m // d) // 16) * 16

    def shift(x, by):
        return lax.ppermute(x, "ctx", [(i, (i + by) % n) for i in range(n)])

    def call(kernel, out_shape, operands, specs, scratch=(), outs=None, mib=40, name=None, flops=0, moved=0):
        single = not isinstance(out_shape, tuple)
        return pl.pallas_call(
            kernel,
            out_shape=out_shape,
            in_specs=specs,
            out_specs=outs or (VMEM if single else (VMEM,) * len(out_shape)),
            scratch_shapes=scratch,
            compiler_params=pltpu.CompilerParams(vmem_limit_bytes=mib << 20),
            cost_estimate=pl.CostEstimate(flops=flops, bytes_accessed=moved, transcendentals=0),
            name=name,
        )(*operands)

    raw = [prefix_keys.reshape(-1, d), prefix_values.reshape(-1, d)]
    slots = span * kv_heads
    chunk = 256 if span % 256 == 0 else span
    batch = 8
    items = rows * (span // chunk)
    smem = pl.BlockSpec(memory_space=pltpu.SMEM)
    split_queries, table = call(
        partial(queries_kernel, kv_heads=kv_heads, chunk=chunk, chunks=span // chunk, pad=2 * batch),
        (jax.ShapeDtypeStruct((kv_heads, m, d), BF16), jax.ShapeDtypeStruct((items + 2 * batch + 1,), jnp.int32)),
        [pltpu.with_memory_space_constraint(x, pltpu.HBM) for x in (lengths, queries)],
        [pl.BlockSpec(memory_space=pltpu.HBM)] * 2,
        scratch=[pltpu.SMEM((rows,), jnp.int32), pltpu.VMEM((rows, heads, d), BF16), pltpu.SemaphoreType.DMA((2,))],
        outs=(VMEM, smem),
        mib=16,
        name="queries",
        moved=4 * m * kv_heads * d,
    )

    def by_head(x):
        return x.reshape(-1, kv_heads, d).transpose(1, 0, 2)

    visiting = [shift(queries, j * cores) for j in range(1, chips)]

    spread = prefix_keys.shape[0]
    flops = 12 * m * kv_heads * spread * d
    moved = 4 * kv_heads * spread * d

    flat = []
    before = ()
    if cores == 2:
        swap = [(i, i ^ 1) for i in range(n)]
        keys, values = [lax.ppermute(x, "ctx", swap) for x in raw]
        keys = by_head(keys)
        weights = call(
            partial(first_kernel, c=c, kv_heads=kv_heads),
            (jax.ShapeDtypeStruct((kv_heads, m, spread), BF16), jax.ShapeDtypeStruct((kv_heads, m, d), F32)),
            (split_queries, keys),
            [VMEM] * 2,
            mib=24,
            name="first",
            flops=3 * flops // 2,
            moved=moved,
        )
        raw, values, weights = lax.optimization_barrier((raw, values, weights))
        flat = [keys, by_head(values)]
        before = (*weights, flat[1])
    raw = [by_head(x) for x in raw]
    operands = (split_queries, *raw, *before)
    own_o, own_l = call(
        partial(own_kernel, c=c, kv_heads=kv_heads),
        (jax.ShapeDtypeStruct((kv_heads, m, d), F32),) * 2,
        operands,
        [VMEM] * len(operands),
        mib=24,
        name="own",
        flops=flops,
        moved=moved,
    )
    flat = [*flat, *raw]
    visiting, own_o, own_l = lax.optimization_barrier((visiting, own_o, own_l))
    message = jax.ShapeDtypeStruct((kv_heads * m + pieces, d), BF16)
    returned = []
    for j, q in enumerate(visiting):
        msg = call(
            partial(other_kernel, c=c, kv_heads=kv_heads, pieces=pieces),
            message,
            (q, *flat),
            [VMEM] * (1 + len(flat)),
            mib=24,
            name="visiting",
            flops=cores * flops,
            moved=cores * moved,
        )
        returned.append(shift(msg, -(j + 1) * cores))
    local = call(
        partial(suffix_kernel, c=c, kv_heads=kv_heads, batch=batch, chunk=chunk),
        (jax.ShapeDtypeStruct((rows, heads, d), F32),) * 2,
        (lengths, table, queries, suffix_keys.reshape(rows, slots, d), suffix_values.reshape(rows, slots, d), own_o, own_l),
        [smem] * 2 + [VMEM] * 5,
        scratch=[
            pltpu.VMEM((items, heads, d), F32),
            pltpu.VMEM((items, heads, d), F32),
        ],
        mib=12,
        name="suffix",
        flops=4 * rows * heads * slots * d,
        moved=4 * rows * slots * d,
    )
    operands = (*local, *returned)
    return call(
        partial(merge_kernel, kv_heads=kv_heads, group=group),
        jax.ShapeDtypeStruct((rows, heads, d), BF16),
        operands,
        [VMEM] * len(operands),
        mib=16,
        name="merge",
    )


def solution(mesh):
    placed = (
        P(("groups", "ctx"), "head", None),
        P(("groups", "ctx"), "head", None),
        P(("groups", "ctx"), "head", None),
        P(("groups", "ctx"), None, "head", None),
        P(("groups", "ctx"), None, "head", None),
        P(("groups", "ctx")),
    )
    return jax.shard_map(
        shards,
        mesh=mesh,
        in_specs=placed,
        out_specs=P(("groups", "ctx"), "head", None),
        check_vma=False,
    )
```
